512 devices in a mesh: member: 16 (over z, core), domain: 32 (over y, x).
Axes of the slice: x: 4, y: 8, z: 8, core: 2. Of those that a mesh axis runs over, the one named last changes fastest.
Arguments:
- initial_realizations: float32 [64, 6, 2048, 256], P('member', None, 'domain'), may hold values from -6 to 6
- land_mask: int32 [2048, 256], P('domain'), may hold values 0 or 1
- obs_index: int32 [32, 16, 256], P('domain', 'member'), may hold values from 0 to 6143
- obs_count: int32 [32, 16], P('domain', 'member'), may hold values from 1 to 256, 2048 in all within a row
- obs_value: float32 [32, 16, 256], P('domain', 'member'), may hold values from -6 to 6
- obs_error: float32 [32, 16, 256], P('domain', 'member'), may hold values from 0.1 to 2
Outputs:
- increments: float32 [64, 6, 2048, 256], P('member', None, 'domain')
The draws below stay inside these ranges and needn't reach their ends.
Inputs may be any that keep to these rules, and one draw needn't show every extreme that they name: `obs_count`: in every tile one region has exactly 256 observations, and the counts of a tile's regions sum to 2048.
All inputs are finite; a program needn't handle non-finite values. No bound on the sum of `land_mask` or of `obs_count` on one device may be relied on, other than what follows from the above.
Results may differ from the reference program's by a relative error of at most 0.0003.
Values sent between devices are 32-bit elements; how exact they have to be, the bound alone decides.
No kernel may reach another device: no remote copies, remote signals or barrier semaphores. Data moves between devices by JAX's collectives and lax.ppermute only.
A program may use at most 192 MiB of HBM per device.

```python
import math
import jax
import jax.numpy as jnp
import numpy as np
from jax import lax

PATCH_WIDTH = 32
PATCHES_EASTWARD = 2
PATCHES_NORTHWARD = 8
VARIABLE_TOTAL = 6
OMAX = 256
NS_ITERS = 8
NY = 256
REGT = 16
NX = 2048
MEMBERSHIP_SIZE = 64
N_DOMAIN = 32


def set_ends(values, stream_key, smallest, high):
    index_at = [jax.random.randint(jax.random.fold_in(stream_key, axis), (), 0, length) for axis, length in enumerate(values.shape)]
    longest = values.shape.index(max(values.shape))
    beside = index_at[:longest] + [(index_at[longest] + 1) % values.shape[longest]] + index_at[longest + 1:]
    return values.at[tuple(index_at)].set(smallest).at[tuple(beside)].set(high)


def shard_levels(rng, extent, split, low, high):
    loudness, own = 1.0, jax.random.fold_in(rng, 6)
    for dim, shards_of in split:
        steps = jnp.exp(jax.random.uniform(jax.random.fold_in(own, dim), (shards_of,), jnp.float32, low / len(split), high / len(split)))
        loudness = loudness * jnp.repeat(steps, extent[dim] // shards_of).reshape([-1 if axis == dim else 1 for axis in range(len(extent))])
    return loudness


def split_up(amount, total, most, lean):
    loads = [(1 << 20) // math.isqrt(rank ** lean) + 1 for rank in range(2, amount + 1)]
    spare, given = total - most - (amount - 1), [1] * (amount - 1)
    while spare > 0:
        candidates = [i for i in range(amount - 1) if given[i] < most]
        mass, left = sum([loads[i] for i in candidates]), spare
        for i in candidates:
            addition = min(most - given[i], max(1, left * loads[i] // mass), spare)
            given[i] = given[i] + addition
            spare = spare - addition
    return np.array([most] + given)


def ragged(stream_key, amount, total, limit, lean):
    if amount == 2:
        one = jax.random.randint(stream_key, (), max(1, total - limit), min(limit, total - 1) + 1)
        return jnp.stack([one, total - one])
    tallies = jnp.asarray(split_up(amount, total, limit, lean), jnp.int32)
    couples = (amount - 1) // 2
    source_of, taker = tallies[1:1 + 2 * couples:2], tallies[2:2 + 2 * couples:2]
    slack = jnp.minimum(source_of - 1, limit - taker)
    passed = jax.random.randint(jax.random.fold_in(stream_key, 1), (couples,), 0, 1 << 20) % (slack + 1)
    tallies = tallies.at[1:1 + 2 * couples:2].set(source_of - passed).at[2:2 + 2 * couples:2].set(taker + passed)
    return tallies[jax.random.permutation(jax.random.fold_in(stream_key, 2), amount)]


def noise(stream_key, dims, scale, most, pieces=(), kind=jnp.bfloat16):
    level = shard_levels(stream_key, dims, pieces, -0.22, 0.18) if pieces else 1.0
    drawn = jax.random.normal(stream_key, dims, jnp.float32) * scale * level
    return jnp.minimum(jnp.maximum(drawn, -most), most).astype(kind)


def setup_inputs(seed: int = 0) -> dict:
    arg_keys = jax.random.split(jax.random.key(seed), 7)
    return {
        "initial_realizations": noise(arg_keys[0], (MEMBERSHIP_SIZE, VARIABLE_TOTAL, NX, NY), 1.0, 6.0, ((0, 16), (2, 32)), jnp.float32),
        "land_mask": set_ends((jax.random.randint(arg_keys[1], (NX, NY), 0, 8) < 7).astype(jnp.int32), jax.random.fold_in(arg_keys[1], 1), 0, 1),
        "obs_index": set_ends(jax.random.randint(arg_keys[2], (N_DOMAIN, REGT, OMAX), 0, VARIABLE_TOTAL * PATCH_WIDTH * PATCH_WIDTH), jax.random.fold_in(arg_keys[2], 1), 0, (VARIABLE_TOTAL * PATCH_WIDTH * PATCH_WIDTH) - 1).astype(jnp.int32),
        "obs_count": jax.vmap(lambda own: ragged(own, REGT, 8 * OMAX, OMAX, 2))(jax.random.split(arg_keys[3], N_DOMAIN)).reshape((N_DOMAIN, REGT)).astype(jnp.int32),
        "obs_value": noise(arg_keys[4], (N_DOMAIN, REGT, OMAX), 1.0, 6.0, ((0, 32), (1, 16)), jnp.float32),
        "obs_error": jnp.clip(jnp.exp(math.log(2.0) - 2.9957323 * jax.random.uniform(arg_keys[5], (N_DOMAIN, REGT, OMAX), jnp.float32) ** shard_levels(arg_keys[5], (N_DOMAIN, REGT, OMAX), ((0, 32), (1, 16)), -0.2, 0.2)), 0.1, 2.0),
    }


COURANT = 0.25
CORIOLIS = 0.1
DEPTH_TOP = 1.0
DEPTH_DEEP = 0.5
STRATIFY = 1.5

def diff_east(field):
    return (field[..., 2:, :] - field[..., :-2, :]) * 0.5

def diff_north(field):
    padded = jnp.pad(field, [(0, 0)] * (field.ndim - 1) + [(1, 1)])
    return (padded[..., 2:] - padded[..., :-2]) * 0.5

def momentum(zonal, merid, pressure, mask_rows):
    zonal_new = (zonal[..., 2:-2, :] + CORIOLIS * merid[..., 2:-2, :] - COURANT * diff_east(pressure)) * mask_rows
    merid_new = (merid[..., 2:-2, :] - CORIOLIS * zonal[..., 2:-2, :] - COURANT * diff_north(pressure)[..., 1:-1, :]) * mask_rows
    return (zonal_new, merid_new)

def advance(state, mask_rows):
    zonal_top = state[..., 0, :, :]
    merid_top = state[..., 1, :, :]
    thick_top = state[..., 2, :, :]
    zonal_deep = state[..., 3, :, :]
    merid_deep = state[..., 4, :, :]
    thick_deep = state[..., 5, :, :]
    new_top = thick_top[..., 1:-1, :] - COURANT * DEPTH_TOP * (diff_east(zonal_top) + diff_north(merid_top)[..., 1:-1, :])
    new_deep = thick_deep[..., 1:-1, :] - COURANT * DEPTH_DEEP * (diff_east(zonal_deep) + diff_north(merid_deep)[..., 1:-1, :])
    press_top = new_top + new_deep
    press_deep = new_top + STRATIFY * new_deep
    zonal_top_new, merid_top_new = momentum(zonal_top, merid_top, press_top, mask_rows)
    zonal_deep_new, merid_deep_new = momentum(zonal_deep, merid_deep, press_deep, mask_rows)
    return jnp.stack([zonal_top_new, merid_top_new, new_top[..., 1:-1, :], zonal_deep_new, merid_deep_new, new_deep[..., 1:-1, :]], axis=-3)

def wrap_pad(state, width):
    return jnp.concatenate([state[..., -width:, :], state, state[..., :width, :]], axis=-2)

def weights(observed, values, errors, count):
    highest = lax.Precision.HIGHEST
    ensemble_size = observed.shape[0]
    obs_mean = lax.optimization_barrier(jnp.mean(observed, axis=0))
    spread = observed - obs_mean
    slots = jnp.arange(observed.shape[1], dtype=jnp.int32)
    precision_w = jnp.where(slots < count, 1.0 / errors, 0.0)
    innovation = values - obs_mean
    scaled = spread * precision_w
    identity = jnp.eye(ensemble_size, dtype=observed.dtype)
    system = (ensemble_size - 1.0) * identity + jnp.dot(scaled, spread.T, precision=highest)
    norm_frob = jnp.sqrt(jnp.sum(system * system))
    root = system / norm_frob
    inverse_root = identity
    for sweep_index in range(NS_ITERS):
        factor = 1.5 * identity - 0.5 * jnp.dot(inverse_root, root, precision=highest)
        root = jnp.dot(root, factor, precision=highest)
        inverse_root = jnp.dot(factor, inverse_root, precision=highest)
    sqrt_inv = inverse_root / jnp.sqrt(norm_frob)
    covariance = jnp.dot(sqrt_inv, sqrt_inv, precision=highest)
    mean_weights = jnp.dot(covariance, jnp.dot(scaled, innovation, precision=highest), precision=highest)
    return mean_weights[:, None] + math.sqrt(ensemble_size - 1.0) * sqrt_inv - identity

def reference(initial_realizations, land_mask, obs_index, obs_count, obs_value, obs_error):
    highest = lax.Precision.HIGHEST
    mask_rows = land_mask.astype(jnp.float32)

    def predict_one_realization(realization_vector):
        for sweep_index in range(2):
            realization_vector = advance(wrap_pad(realization_vector, 2), mask_rows)
        return realization_vector
    predict_realizations = lax.map(predict_one_realization, initial_realizations)
    patch_tiling = predict_realizations.reshape(MEMBERSHIP_SIZE, VARIABLE_TOTAL, N_DOMAIN, PATCHES_EASTWARD, PATCH_WIDTH, PATCHES_NORTHWARD, PATCH_WIDTH)
    patch_tiling = patch_tiling.transpose(2, 3, 5, 0, 1, 4, 6).reshape(N_DOMAIN * REGT, MEMBERSHIP_SIZE, VARIABLE_TOTAL * PATCH_WIDTH * PATCH_WIDTH)

    def analyse(items):
        block, chosen, count, values, errors = items
        observed = jnp.take(block, chosen, axis=1)
        matrix = weights(observed, values, errors, count)
        deviations = block - lax.optimization_barrier(jnp.mean(block, axis=0))
        return jnp.dot(matrix.T, deviations, precision=highest)
    result = lax.map(analyse, (patch_tiling, obs_index.reshape(-1, OMAX), obs_count.reshape(-1), obs_value.reshape(-1, OMAX), obs_error.reshape(-1, OMAX)))
    result = result.reshape(N_DOMAIN, PATCHES_EASTWARD, PATCHES_NORTHWARD, MEMBERSHIP_SIZE, VARIABLE_TOTAL, PATCH_WIDTH, PATCH_WIDTH)
    result = result.transpose(3, 4, 0, 1, 5, 2, 6).reshape(MEMBERSHIP_SIZE, VARIABLE_TOTAL, NX, NY)
    return result * mask_rows
```

```python
import math

import jax
import jax.numpy as jnp
from jax import lax
from jax.experimental import pallas as pl
from jax.experimental.pallas import tpu as pltpu
from jax.sharding import PartitionSpec as P

NS_ITERS = 8
CORIOLIS = 0.1
STRATIFY = 1.5
HALO = 4
VMEM_LIMIT = 48 * 1024 * 1024


def call(kernel, out_shape, n_in, scratch=(), aliases=None, flops=1000000, nbytes=3000000):
    whole = pl.BlockSpec(memory_space=pltpu.VMEM)
    return pl.pallas_call(
        kernel,
        out_shape=out_shape,
        in_specs=[whole] * n_in,
        out_specs=jax.tree.map(lambda _: whole, out_shape),
        scratch_shapes=list(scratch),
        input_output_aliases=aliases or {},
        compiler_params=pltpu.CompilerParams(vmem_limit_bytes=VMEM_LIMIT),
        cost_estimate=pl.CostEstimate(flops=flops, bytes_accessed=nbytes, transcendentals=0),
    )


def east(field):
    rows = field.shape[0]
    return pltpu.roll(field, rows - 1, 0) - pltpu.roll(field, 1, 0)


def north(field, first, last):
    cols = field.shape[1]
    ahead = jnp.where(last, 0.0, pltpu.roll(field, cols - 1, 1))
    behind = jnp.where(first, 0.0, pltpu.roll(field, 1, 1))
    return ahead - behind


def step(state, mask, first, last):
    u1, v1, h1, u2, v2, h2 = state
    h1 = h1 - 0.125 * (east(u1) + north(v1, first, last))
    h2 = h2 - 0.0625 * (east(u2) + north(v2, first, last))
    p1 = h1 + h2
    p2 = h1 + STRATIFY * h2
    u1n = (u1 + CORIOLIS * v1 - 0.125 * east(p1)) * mask
    v1n = (v1 - CORIOLIS * u1 - 0.125 * north(p1, first, last)) * mask
    u2n = (u2 + CORIOLIS * v2 - 0.125 * east(p2)) * mask
    v2n = (v2 - CORIOLIS * u2 - 0.125 * north(p2, first, last)) * mask
    return (u1n, v1n, h1, u2n, v2n, h2)


def forecast(state, mask):
    lane = lax.broadcasted_iota(jnp.int32, mask.shape, 1)
    first = lane == 0
    last = lane == mask.shape[1] - 1
    for _ in range(2):
        state = step(state, mask, first, last)
    return state


def swap_blocks(x, low, even):
    y0 = jnp.where(low, x[0], pltpu.roll(x[2], 64, 1))
    y2 = jnp.where(low, pltpu.roll(x[0], 64, 1), x[2])
    y1 = jnp.where(low, x[1], pltpu.roll(x[3], 64, 1))
    y3 = jnp.where(low, pltpu.roll(x[1], 64, 1), x[3])
    z0 = jnp.where(even, y0, pltpu.roll(y1, 32, 1))
    z1 = jnp.where(even, pltpu.roll(y0, 96, 1), y1)
    z2 = jnp.where(even, y2, pltpu.roll(y3, 32, 1))
    z3 = jnp.where(even, pltpu.roll(y2, 96, 1), y3)
    return (z0, z1, z2, z3)


def lane_tests():
    lane = lax.broadcasted_iota(jnp.int32, (8, 128), 1)
    return lane < 64, (lane // 32) % 2 == 0, lane


def edges_kernel(state, land, low_out, high_out):
    low_out[24] = land[60:64, :].astype(jnp.float32)
    high_out[24] = land[0:4, :].astype(jnp.float32)
    for m in range(4):
        for f in range(6):
            low_out[6 * m + f] = state[m, f, 60:64, :]
            high_out[6 * m + f] = state[m, f, 0:4, :]


def interior_kernel(state, land, packed):
    low, even, _ = lane_tests()
    mask = land[...].astype(jnp.float32)

    def one(m, carry):
        fields = forecast(tuple(state[m, f] for f in range(6)), mask)
        for f in range(6):
            for qx in range(2):
                for g in range(2):
                    x = [
                        fields[f][qx * 32 + 8 * a : qx * 32 + 8 * a + 8, g * 128 : g * 128 + 128]
                        for a in range(4)
                    ]
                    z = swap_blocks(x, low, even)
                    for b in range(4):
                        packed[qx * 8 + g * 4 + b, m, f] = z[b]
        return carry

    lax.fori_loop(0, 4, one, 0)


def border_kernel(state, land, from_low, from_high, inner, packed):
    _, _, lane = lane_tests()
    pad = jnp.zeros((8 - HALO, 256), jnp.float32)
    mask_low = jnp.concatenate([pad, from_low[24], land[0:16, :].astype(jnp.float32)], axis=0)
    mask_high = jnp.concatenate([land[48:64, :].astype(jnp.float32), from_high[24], pad], axis=0)

    def one(m, carry):
        for qx in range(2):
            if qx == 0:
                begin = tuple(
                    jnp.concatenate([pad, from_low[6 * m + f], state[m, f, 0:16, :]], axis=0)
                    for f in range(6)
                )
                fields = forecast(begin, mask_low)
                mine = lane < 32
            else:
                begin = tuple(
                    jnp.concatenate([state[m, f, 48:64, :], from_high[6 * m + f], pad], axis=0)
                    for f in range(6)
                )
                fields = forecast(begin, mask_high)
                mine = lane >= 96
            for f in range(6):
                for g in range(2):
                    x = fields[f][8:16, g * 128 : g * 128 + 128]
                    for b in range(4):
                        turn = ((0 if qx == 0 else 3) - b) % 4 * 32
                        moved = pltpu.roll(x, turn, 1) if turn else x
                        q = qx * 8 + g * 4 + b
                        packed[q, m, f] = jnp.where(mine, moved, inner[q, m, f])
        return carry

    lax.fori_loop(0, 4, one, 0)


def analysis_kernel(x_ref, index, count, values, errors, out_ref, dev_ref):
    highest = lax.Precision.HIGHEST
    members = 64
    chosen = index[...]
    entry_row = ((chosen >> 10) << 3) + ((chosen >> 5) & 7)
    entry_lane = (((chosen >> 8) & 3) << 5) + (chosen & 31)
    rows_of = [jnp.broadcast_to(entry_row[:, 128 * i : 128 * i + 128], (members, 128)) for i in range(2)]
    lanes_of = [jnp.broadcast_to(entry_lane[:, 128 * i : 128 * i + 128], (members, 128)) for i in range(2)]

    def scan(r, acc):
        x = x_ref[pl.ds(r, members, stride=48), :]
        dev_ref[r] = x - jnp.sum(x, axis=0, keepdims=True) * (1.0 / members)
        return tuple(
            jnp.where(rows_of[i] == r, jnp.take_along_axis(x, lanes_of[i], axis=1), acc[i])
            for i in range(2)
        )

    zero = jnp.zeros((members, 128), jnp.float32)
    observed = jnp.concatenate(lax.fori_loop(0, 48, scan, (zero, zero)), axis=1)
    obs_mean = jnp.sum(observed, axis=0, keepdims=True) * (1.0 / members)
    spread = observed - obs_mean
    slots = lax.broadcasted_iota(jnp.int32, (1, 256), 1)
    weight = jnp.where(slots < count[0, 0], 1.0 / errors[...], 0.0)
    innovation = values[...] - obs_mean
    scaled = spread * weight
    eye = (
        lax.broadcasted_iota(jnp.int32, (members, members), 0)
        == lax.broadcasted_iota(jnp.int32, (members, members), 1)
    ).astype(jnp.float32)

    def dot(a, b):
        return jnp.dot(a, b, precision=highest, preferred_element_type=jnp.float32)

    system = (members - 1.0) * eye + lax.dot_general(
        scaled, spread, (((1,), (1,)), ((), ())), precision=highest, preferred_element_type=jnp.float32
    )
    total = jnp.sum(jnp.sum(system * system, axis=1, keepdims=True), axis=0, keepdims=True)
    norm = jnp.sqrt(total)
    root = system / norm
    inverse = eye
    for sweep in range(NS_ITERS):
        factor = 1.5 * eye - 0.5 * (root if sweep == 0 else dot(inverse, root))
        if sweep < NS_ITERS - 1:
            root = dot(root, factor)
        inverse = factor if sweep == 0 else dot(factor, inverse)
    sqrt_inv = inverse / jnp.sqrt(norm)
    moved = jnp.sum(scaled * innovation, axis=1, keepdims=True)
    half = jnp.sum(sqrt_inv * moved, axis=0, keepdims=True)
    mean_weights = jnp.sum(sqrt_inv * half, axis=1, keepdims=True)
    transform = mean_weights + math.sqrt(members - 1.0) * sqrt_inv - eye
    flipped = transform.T

    def apply(r, carry):
        out_ref[pl.ds(r, members, stride=48), :] = dot(flipped, dev_ref[r])
        return carry

    lax.fori_loop(0, 48, apply, 0)


def unpack_kernel(packed, land, out):
    low, even, _ = lane_tests()
    mask = land[...].astype(jnp.float32)

    def one(m, carry):
        for f in range(6):
            for qx in range(2):
                for g in range(2):
                    x = [packed[qx * 8 + g * 4 + b, m, f] for b in range(4)]
                    z = swap_blocks(x, low, even)
                    for a in range(4):
                        rows = slice(qx * 32 + 8 * a, qx * 32 + 8 * a + 8)
                        cols = slice(g * 128, g * 128 + 128)
                        out[m, f, rows, cols] = z[a] * mask[rows, cols]
        return carry

    lax.fori_loop(0, 4, one, 0)


def shape(*dims):
    return jax.ShapeDtypeStruct(dims, jnp.float32)


def local(initial_realizations, land_mask, obs_index, obs_count, obs_value, obs_error):
    to_high, to_low = call(edges_kernel, [shape(25, HALO, 256)] * 2, 2, nbytes=200000)(
        initial_realizations, land_mask
    )
    count = lax.axis_size("domain")
    forward = [(i, (i + 1) % count) for i in range(count)]
    backward = [(target, source) for source, target in forward]
    from_low = lax.ppermute(to_high, "domain", forward)
    from_high = lax.ppermute(to_low, "domain", backward)
    packed = call(interior_kernel, shape(16, 4, 6, 8, 128), 2)(initial_realizations, land_mask)
    packed = call(border_kernel, shape(16, 4, 6, 8, 128), 5, aliases={4: 0})(
        initial_realizations, land_mask, from_low, from_high, packed
    )
    grouped = lax.all_to_all(packed, "member", split_axis=0, concat_axis=0, tiled=True)
    whole = pl.BlockSpec(memory_space=pltpu.VMEM)
    increment = pl.pallas_call(
        analysis_kernel,
        out_shape=shape(3072, 128),
        in_specs=[whole, whole, pl.BlockSpec(memory_space=pltpu.SMEM), whole, whole],
        out_specs=whole,
        scratch_shapes=[pltpu.VMEM((48, 64, 128), jnp.float32)],
        compiler_params=pltpu.CompilerParams(vmem_limit_bytes=VMEM_LIMIT),
    )(grouped.reshape(3072, 128), obs_index[0], obs_count, obs_value[0], obs_error[0])
    returned = lax.all_to_all(
        increment.reshape(16, 4, 6, 8, 128), "member", split_axis=0, concat_axis=0, tiled=True
    )
    return call(unpack_kernel, shape(4, 6, 64, 256), 2)(returned, land_mask)


def solution(mesh):
    in_specs = (
        P("member", None, "domain", None),
        P("domain", None),
        P("domain", "member", None),
        P("domain", "member"),
        P("domain", "member", None),
        P("domain", "member", None),
    )
    out_specs = P("member", None, "domain", None)
    return jax.shard_map(local, mesh=mesh, in_specs=in_specs, out_specs=out_specs, check_vma=False)
```

```python
import math

import jax
import jax.numpy as jnp
from jax import lax
from jax.experimental import pallas as pl
from jax.experimental.pallas import tpu as pltpu
from jax.sharding import PartitionSpec as P

NS_ITERS = 8
CORIOLIS = 0.1
STRATIFY = 1.5
HALO = 4
SCAN = 8
APPLY = 8
VMEM_LIMIT = 48 * 1024 * 1024


def call(kernel, out_shape, n_in, scratch=(), aliases=None, flops=1000000, nbytes=3000000):
    whole = pl.BlockSpec(memory_space=pltpu.VMEM)
    return pl.pallas_call(
        kernel,
        out_shape=out_shape,
        in_specs=[whole] * n_in,
        out_specs=jax.tree.map(lambda _: whole, out_shape),
        scratch_shapes=list(scratch),
        input_output_aliases=aliases or {},
        compiler_params=pltpu.CompilerParams(vmem_limit_bytes=VMEM_LIMIT),
        cost_estimate=pl.CostEstimate(flops=flops, bytes_accessed=nbytes, transcendentals=0),
    )


def east(field):
    rows = field.shape[0]
    return pltpu.roll(field, rows - 1, 0) - pltpu.roll(field, 1, 0)


def north(field, first, last):
    cols = field.shape[1]
    ahead = jnp.where(last, 0.0, pltpu.roll(field, cols - 1, 1))
    behind = jnp.where(first, 0.0, pltpu.roll(field, 1, 1))
    return ahead - behind


def step(state, mask, first, last):
    u1, v1, h1, u2, v2, h2 = state
    h1 = h1 - 0.125 * (east(u1) + north(v1, first, last))
    h2 = h2 - 0.0625 * (east(u2) + north(v2, first, last))
    p1 = h1 + h2
    p2 = h1 + STRATIFY * h2
    u1n = (u1 + CORIOLIS * v1 - 0.125 * east(p1)) * mask
    v1n = (v1 - CORIOLIS * u1 - 0.125 * north(p1, first, last)) * mask
    u2n = (u2 + CORIOLIS * v2 - 0.125 * east(p2)) * mask
    v2n = (v2 - CORIOLIS * u2 - 0.125 * north(p2, first, last)) * mask
    return (u1n, v1n, h1, u2n, v2n, h2)


def forecast(state, mask):
    lane = lax.broadcasted_iota(jnp.int32, mask.shape, 1)
    first = lane == 0
    last = lane == mask.shape[1] - 1
    for _ in range(2):
        state = step(state, mask, first, last)
    return state


def swap_blocks(groups):
    lane = lax.broadcasted_iota(jnp.int32, (8, 128), 1)
    low = lane < 64
    even = (lane & 32) == 0
    half = [
        (
            jnp.where(low, x[0], pltpu.roll(x[2], 64, 1)),
            jnp.where(low, x[1], pltpu.roll(x[3], 64, 1)),
            jnp.where(low, pltpu.roll(x[0], 64, 1), x[2]),
            jnp.where(low, pltpu.roll(x[1], 64, 1), x[3]),
        )
        for x in groups
    ]
    return [
        (
            jnp.where(even, y[0], pltpu.roll(y[1], 32, 1)),
            jnp.where(even, pltpu.roll(y[0], 96, 1), y[1]),
            jnp.where(even, y[2], pltpu.roll(y[3], 32, 1)),
            jnp.where(even, pltpu.roll(y[2], 96, 1), y[3]),
        )
        for y in half
    ]


BLOCKS = [(f, qx, g) for f in range(6) for qx in range(2) for g in range(2)]


def tile_at(qx, g, a):
    row = qx * 32 + 8 * a
    return slice(row, row + 8), slice(g * 128, g * 128 + 128)


def edges_kernel(top, bottom, land_top, land_bottom, low_out, high_out):
    low_out[24] = land_bottom[8 - HALO :, :].astype(jnp.float32)
    high_out[24] = land_top[:HALO, :].astype(jnp.float32)
    for m in range(4):
        for f in range(6):
            low_out[6 * m + f] = bottom[m, f, 8 - HALO :, :]
            high_out[6 * m + f] = top[m, f, :HALO, :]


def forecast_kernel(state, land, from_low, from_high, packed):
    mask = jnp.concatenate([land[...].astype(jnp.float32), from_high[24], from_low[24]], axis=0)

    def one(m, carry):
        begin = tuple(
            jnp.concatenate([state[m, f], from_high[6 * m + f], from_low[6 * m + f]], axis=0)
            for f in range(6)
        )
        fields = forecast(begin, mask)
        for i in range(0, len(BLOCKS), 12):
            todo = BLOCKS[i : i + 12]
            tiles = swap_blocks([[fields[f][tile_at(qx, g, a)] for a in range(4)] for f, qx, g in todo])
            for (f, qx, g), z in zip(todo, tiles):
                for b in range(4):
                    packed[qx * 8 + g * 4 + b, m, f] = z[b]
        return carry

    lax.fori_loop(0, 4, one, 0)


def analysis_kernel(x_ref, index, count, values, errors, out_ref, dev_ref):
    highest = lax.Precision.HIGHEST
    members = 64
    chosen = index[...]
    entry_row = ((chosen >> 10) << 3) + ((chosen >> 5) & 7)
    entry_lane = (((chosen >> 8) & 3) << 5) + (chosen & 31)
    rows_of = [jnp.broadcast_to(entry_row[:, 128 * i : 128 * i + 128], (members, 128)) for i in range(2)]
    lanes_of = [jnp.broadcast_to(entry_lane[:, 128 * i : 128 * i + 128], (members, 128)) for i in range(2)]

    def scan(block, acc):
        tiles = [x_ref[pl.ds(block * SCAN + i, members, stride=48), :] for i in range(SCAN)]
        for i in range(SCAN):
            acc = tuple(
                jnp.where(
                    rows_of[half] == block * SCAN + i,
                    jnp.take_along_axis(tiles[i], lanes_of[half], axis=1),
                    acc[half],
                )
                for half in range(2)
            )
        return acc

    def split(rows):
        tiles = [x_ref[pl.ds(r, members, stride=48), :] for r in rows]
        for r, x in zip(rows, tiles):
            dev = x - jnp.sum(x, axis=0, keepdims=True) * (1.0 / members)
            high = dev.astype(jnp.bfloat16)
            dev_ref[r, 0:members, :] = high
            dev_ref[r, members:, :] = (dev - high.astype(jnp.float32)).astype(jnp.bfloat16)

    zero = jnp.zeros((members, 128), jnp.float32)
    observed = jnp.concatenate(lax.fori_loop(0, 48 // SCAN, scan, (zero, zero)), axis=1)
    obs_mean = jnp.sum(observed, axis=0, keepdims=True) * (1.0 / members)
    spread = observed - obs_mean
    slots = lax.broadcasted_iota(jnp.int32, (1, 256), 1)
    weight = jnp.where(slots < count[0, 0], 1.0 / errors[...], 0.0)
    innovation = values[...] - obs_mean
    scaled = spread * weight
    eye = (
        lax.broadcasted_iota(jnp.int32, (members, members), 0)
        == lax.broadcasted_iota(jnp.int32, (members, members), 1)
    ).astype(jnp.float32)

    def dot(a, b):
        return jnp.dot(a, b, precision=highest, preferred_element_type=jnp.float32)

    system = (members - 1.0) * eye + lax.dot_general(
        scaled, spread, (((1,), (1,)), ((), ())), precision=highest, preferred_element_type=jnp.float32
    )
    total = jnp.sum(jnp.sum(system * system, axis=1, keepdims=True), axis=0, keepdims=True)
    norm = jnp.sqrt(total)
    root = system / norm
    inverse = eye
    for sweep in range(NS_ITERS):
        split(range(6 * sweep, 6 * sweep + 6))
        factor = 1.5 * eye - 0.5 * (root if sweep == 0 else dot(inverse, root))
        if sweep < NS_ITERS - 1:
            root = dot(root, factor)
        inverse = factor if sweep == 0 else dot(factor, inverse)
    sqrt_inv = inverse / jnp.sqrt(norm)
    moved = jnp.sum(scaled * innovation, axis=1, keepdims=True)
    half = jnp.sum(sqrt_inv * moved, axis=0, keepdims=True)
    mean_weights = jnp.sum(sqrt_inv * half, axis=1, keepdims=True)
    transform = mean_weights + math.sqrt(members - 1.0) * sqrt_inv - eye
    flipped = transform.T
    high = flipped.astype(jnp.bfloat16)
    low = (flipped - high.astype(jnp.float32)).astype(jnp.bfloat16)
    left = jnp.concatenate([high, high, low, low], axis=1)

    def apply(block, carry):
        first = block * (2 * APPLY)
        results = []
        for i in range(APPLY):
            pair = jnp.concatenate([dev_ref[first + 2 * i], dev_ref[first + 2 * i + 1]], axis=1)
            right = jnp.concatenate([pair, pair], axis=0)
            results.append(jnp.dot(left, right, preferred_element_type=jnp.float32))
        for i in range(APPLY):
            for j in range(2):
                out_ref[pl.ds(first + 2 * i + j, members, stride=48), :] = results[i][:, 128 * j : 128 * j + 128]
        return carry

    lax.fori_loop(0, 24 // APPLY, apply, 0)


def unpack_kernel(packed, land, out):
    mask = land[...].astype(jnp.float32)

    def one(m, carry):
        for i in range(0, len(BLOCKS), 12):
            todo = BLOCKS[i : i + 12]
            tiles = swap_blocks([[packed[qx * 8 + g * 4 + b, m, f] for b in range(4)] for f, qx, g in todo])
            for (f, qx, g), z in zip(todo, tiles):
                for a in range(4):
                    rows, cols = tile_at(qx, g, a)
                    out[m, f, rows, cols] = z[a] * mask[rows, cols]
        return carry

    lax.fori_loop(0, 4, one, 0)


def shape(*dims):
    return jax.ShapeDtypeStruct(dims, jnp.float32)


def local(initial_realizations, land_mask, obs_index, obs_count, obs_value, obs_error):
    payload = pl.BlockSpec((25, HALO, 256), lambda i: (0, 0, 0))
    to_high, to_low = pl.pallas_call(
        edges_kernel,
        grid=(1,),
        out_shape=[shape(25, HALO, 256)] * 2,
        in_specs=[
            pl.BlockSpec((4, 6, 8, 256), lambda i: (0, 0, 0, 0)),
            pl.BlockSpec((4, 6, 8, 256), lambda i: (0, 0, 7, 0)),
            pl.BlockSpec((8, 256), lambda i: (0, 0)),
            pl.BlockSpec((8, 256), lambda i: (7, 0)),
        ],
        out_specs=[payload, payload],
        cost_estimate=pl.CostEstimate(flops=100000, bytes_accessed=800000, transcendentals=0),
    )(initial_realizations, initial_realizations, land_mask, land_mask)
    count = lax.axis_size("domain")
    forward = [(i, (i + 1) % count) for i in range(count)]
    backward = [(target, source) for source, target in forward]
    from_low = lax.ppermute(to_high, "domain", forward)
    from_high = lax.ppermute(to_low, "domain", backward)
    packed = call(forecast_kernel, shape(16, 4, 6, 8, 128), 4)(
        initial_realizations, land_mask, from_low, from_high
    )
    grouped = lax.all_to_all(packed, "member", split_axis=0, concat_axis=0, tiled=True)
    whole = pl.BlockSpec(memory_space=pltpu.VMEM)
    increment = pl.pallas_call(
        analysis_kernel,
        out_shape=shape(3072, 128),
        in_specs=[whole, whole, pl.BlockSpec(memory_space=pltpu.SMEM), whole, whole],
        out_specs=whole,
        scratch_shapes=[pltpu.VMEM((48, 128, 128), jnp.bfloat16)],
        compiler_params=pltpu.CompilerParams(vmem_limit_bytes=VMEM_LIMIT),
    )(grouped.reshape(3072, 128), obs_index[0], obs_count, obs_value[0], obs_error[0])
    returned = lax.all_to_all(
        increment.reshape(16, 4, 6, 8, 128), "member", split_axis=0, concat_axis=0, tiled=True
    )
    return call(unpack_kernel, shape(4, 6, 64, 256), 2)(returned, land_mask)


def solution(mesh):
    in_specs = (
        P("member", None, "domain", None),
        P("domain", None),
        P("domain", "member", None),
        P("domain", "member"),
        P("domain", "member", None),
        P("domain", "member", None),
    )
    out_specs = P("member", None, "domain", None)
    return jax.shard_map(local, mesh=mesh, in_specs=in_specs, out_specs=out_specs, check_vma=False)
```

```python
import math

import jax
import jax.numpy as jnp
from jax import lax
from jax.experimental import pallas as pl
from jax.experimental.pallas import tpu as pltpu
from jax.sharding import PartitionSpec as P

NS_ITERS = 8
CORIOLIS = 0.1
STRATIFY = 1.5
HALO = 4
SCAN = 14
VMEM_LIMIT = 48 * 1024 * 1024
WHOLE_VMEM = 62 * 1024 * 1024


def east(field):
    rows = field.shape[0]
    return pltpu.roll(field, rows - 1, 0) - pltpu.roll(field, 1, 0)


def north(field, first, last):
    cols = field.shape[1]
    ahead = jnp.where(last, 0.0, pltpu.roll(field, cols - 1, 1))
    behind = jnp.where(first, 0.0, pltpu.roll(field, 1, 1))
    return ahead - behind


def step(state, mask, first, last):
    u1, v1, h1, u2, v2, h2 = state
    h1 = h1 - 0.125 * (east(u1) + north(v1, first, last))
    h2 = h2 - 0.0625 * (east(u2) + north(v2, first, last))
    p1 = h1 + h2
    p2 = h1 + STRATIFY * h2
    u1n = (u1 + CORIOLIS * v1 - 0.125 * east(p1)) * mask
    v1n = (v1 - CORIOLIS * u1 - 0.125 * north(p1, first, last)) * mask
    u2n = (u2 + CORIOLIS * v2 - 0.125 * east(p2)) * mask
    v2n = (v2 - CORIOLIS * u2 - 0.125 * north(p2, first, last)) * mask
    return (u1n, v1n, h1, u2n, v2n, h2)


def forecast(state, mask):
    lane = lax.broadcasted_iota(jnp.int32, mask.shape, 1)
    first = lane == 0
    last = lane == mask.shape[1] - 1
    for _ in range(2):
        state = step(state, mask, first, last)
    return state


def swap_blocks(groups):
    lane = lax.broadcasted_iota(jnp.int32, (8, 128), 1)
    low = lane < 64
    even = (lane & 32) == 0
    half = [
        (
            jnp.where(low, x[0], pltpu.roll(x[2], 64, 1)),
            jnp.where(low, x[1], pltpu.roll(x[3], 64, 1)),
            jnp.where(low, pltpu.roll(x[0], 64, 1), x[2]),
            jnp.where(low, pltpu.roll(x[1], 64, 1), x[3]),
        )
        for x in groups
    ]
    return [
        (
            jnp.where(even, y[0], pltpu.roll(y[1], 32, 1)),
            jnp.where(even, pltpu.roll(y[0], 96, 1), y[1]),
            jnp.where(even, y[2], pltpu.roll(y[3], 32, 1)),
            jnp.where(even, pltpu.roll(y[2], 96, 1), y[3]),
        )
        for y in half
    ]


BLOCKS = [(f, qx, g) for f in range(6) for qx in range(2) for g in range(2)]
INNER = 7
INNER_ROWS = 6 * INNER


def edges_kernel(state, land, low_out, high_out, top, bottom, land_top, land_bottom, sems):
    copies = [
        pltpu.make_async_copy(state.at[:, :, 0:8, :], top, sems.at[0]),
        pltpu.make_async_copy(state.at[:, :, 56:64, :], bottom, sems.at[1]),
        pltpu.make_async_copy(land.at[0:8, :], land_top, sems.at[2]),
        pltpu.make_async_copy(land.at[56:64, :], land_bottom, sems.at[3]),
    ]
    for copy in copies:
        copy.start()
    for copy in copies:
        copy.wait()
    low_out[24] = land_bottom[8 - HALO :, :].astype(jnp.float32)
    high_out[24] = land_top[:HALO, :].astype(jnp.float32)
    for m in range(4):
        for f in range(6):
            low_out[6 * m + f] = bottom[m, f, 8 - HALO :, :]
            high_out[6 * m + f] = top[m, f, :HALO, :]


CUTS = (0, 40, 80, 120, 168)


def inner_kernel(state, land, out, begin, land_ref, packed, fields_ref, sems):
    arrive = [pltpu.make_async_copy(land, land_ref, sems.at[0])]
    arrive += [pltpu.make_async_copy(state.at[m], begin.at[m], sems.at[1 + m]) for m in range(4)]
    leave = [
        pltpu.make_async_copy(
            packed.at[:, pl.ds(CUTS[m], CUTS[m + 1] - CUTS[m]), :],
            out.at[:, pl.ds(CUTS[m], CUTS[m + 1] - CUTS[m]), :],
            sems.at[5 + m],
        )
        for m in range(4)
    ]
    for copy in arrive:
        copy.start()
    arrive[0].wait()
    mask = land_ref[...].astype(jnp.float32)
    for m in range(4):
        arrive[1 + m].wait()
        fields = forecast(tuple(begin[m, f] for f in range(6)), mask)
        for f in range(6):
            for g in range(2):
                fields_ref[m % 2, f, g] = fields[f][:, 128 * g : 128 * g + 128]
        for i in range(0, len(BLOCKS), 12):
            todo = BLOCKS[i : i + 12]
            tiles = swap_blocks(
                [
                    [fields_ref[m % 2, f, g, pl.ds((4, 32)[qx] + a, 8, stride=4), :] for a in range(4)]
                    for f, qx, g in todo
                ]
            )
            for (f, qx, g), z in zip(todo, tiles):
                row = m * INNER_ROWS + f * INNER
                for b in range(4):
                    packed[qx * 8 + g * 4 + b, row : row + INNER, :] = z[b][0:INNER]
        leave[m].start()
    for copy in leave:
        copy.wait()


def outer_kernel(state, land, from_low, from_high, packed, fields_ref):
    mask = jnp.concatenate(
        [
            land[0:16, :].astype(jnp.float32),
            land[48:64, :].astype(jnp.float32),
            from_high[24],
            from_low[24],
        ],
        axis=0,
    )

    def one(m, carry):
        begin = tuple(
            jnp.concatenate(
                [state[m, f, 0:16, :], state[m, f, 48:64, :], from_high[6 * m + f], from_low[6 * m + f]],
                axis=0,
            )
            for f in range(6)
        )
        fields = forecast(begin, mask)
        for f in range(6):
            for g in range(2):
                cols = slice(128 * g, 128 * g + 128)
                sides = jnp.concatenate([fields[f][0:4, cols], fields[f][28:32, cols]], axis=0)
                fields_ref[g, pl.ds(pl.multiple_of((6 * m + f) * 8, 8), 8), :] = sides
        return carry

    lax.fori_loop(0, 4, one, 0)
    todo = [(i, qx, g) for i in range(3) for qx in range(2) for g in range(2)]
    tiles = swap_blocks(
        [
            [fields_ref[g, pl.ds(64 * i + 4 * qx + a, 8, stride=8), :] for a in range(4)]
            for i, qx, g in todo
        ]
    )
    for (i, qx, g), z in zip(todo, tiles):
        for b in range(4):
            packed[qx * 8 + g * 4 + b, 8 * i : 8 * i + 8, :] = z[b]


def places(index, members):
    chosen = index[...]
    side = lax.axis_index("member") // 8
    field = chosen >> 10
    group = ((chosen >> 7) + side) & 7
    row = jnp.where(group == 0, INNER_ROWS + field, field * INNER + group - 1)
    lane = chosen & 127
    halves = [slice(0, 128), slice(128, 256)]
    return (
        [jnp.broadcast_to(row[:, half], (members, 128)) for half in halves],
        [jnp.broadcast_to(lane[:, half], (members, 128)) for half in halves],
    )


def pick(tile, r, rows_of, lanes_of, acc):
    return tuple(
        jnp.where(rows_of[half] == r, jnp.take_along_axis(tile, lanes_of[half], axis=1), acc[half])
        for half in range(2)
    )


def split(x):
    members = x.shape[0]
    dev = x - jnp.sum(x, axis=0, keepdims=True) * (1.0 / members)
    high = dev.astype(jnp.bfloat16)
    return high, (dev - high.astype(jnp.float32)).astype(jnp.bfloat16)


def gather_kernel(x_ref, index, observed, dev_ref):
    members = 64
    rows_of, lanes_of = places(index, members)

    def scan(block, acc):
        rows = [block * SCAN + i for i in range(SCAN)]
        tiles = [x_ref[pl.ds(r, members, stride=INNER_ROWS), :] for r in rows]
        for r, tile in zip(rows, tiles):
            acc = pick(tile, r, rows_of, lanes_of, acc)
        for r, tile in zip(rows, tiles):
            high, low = split(tile)
            dev_ref[r, 0:members, :] = high
            dev_ref[r, members:, :] = low
        return acc

    zero = jnp.zeros((members, 128), jnp.float32)
    acc = lax.fori_loop(0, INNER_ROWS // SCAN, scan, (zero, zero))
    observed[:, 0:128] = acc[0]
    observed[:, 128:256] = acc[1]


def analysis_kernel(
    x_ref, picked, dev_ref, index, count, values, errors, out, out_ref, outer_ref, sems
):
    highest = lax.Precision.HIGHEST
    members = 64
    rows_of, lanes_of = places(index, members)
    acc = (picked[:, 0:128], picked[:, 128:256])
    for f in range(6):
        tile = x_ref[pl.ds(f, members, stride=6), :]
        acc = pick(tile, INNER_ROWS + f, rows_of, lanes_of, acc)
        high, low = split(tile)
        outer_ref[f, 0:members, :] = high
        outer_ref[f, members:, :] = low
    observed = jnp.concatenate(acc, axis=1)
    obs_mean = jnp.sum(observed, axis=0, keepdims=True) * (1.0 / members)
    spread = observed - obs_mean
    slots = lax.broadcasted_iota(jnp.int32, (1, 256), 1)
    weight = jnp.where(slots < count[...], 1.0 / errors[...], 0.0)
    innovation = values[...] - obs_mean
    scaled = spread * weight
    eye = (
        lax.broadcasted_iota(jnp.int32, (members, members), 0)
        == lax.broadcasted_iota(jnp.int32, (members, members), 1)
    ).astype(jnp.float32)

    def parts(a):
        high = a.astype(jnp.bfloat16)
        return high, (a - high.astype(jnp.float32)).astype(jnp.bfloat16)

    def times(a, b):
        left = jnp.concatenate(a, axis=1)
        right = jnp.concatenate(b + b, axis=0)
        return jnp.dot(left, right, preferred_element_type=jnp.float32)

    gram = lax.dot_general(
        scaled, spread, (((1,), (1,)), ((), ())), precision=highest, preferred_element_type=jnp.float32
    )
    system = (members - 1.0) * eye + gram
    total = jnp.sum(jnp.sum(system * system, axis=1, keepdims=True), axis=0, keepdims=True)
    norm = jnp.sqrt(total)
    twice = jnp.concatenate([eye, eye], axis=1)
    root = jnp.concatenate([system, system], axis=1) / norm
    inverse = twice
    for sweep in range(NS_ITERS):
        root_parts, inverse_parts = parts(root), parts(inverse)
        factor = 1.5 * twice - 0.5 * (root if sweep == 0 else times(inverse_parts, root_parts))
        factor_parts = parts(factor)
        if sweep < NS_ITERS - 1:
            root = times(root_parts, factor_parts)
        inverse = factor if sweep == 0 else times(factor_parts, inverse_parts)
    sqrt_inv = inverse[:, 0:members] / jnp.sqrt(norm)
    moved = jnp.sum(scaled * innovation, axis=1, keepdims=True)
    half = jnp.sum(sqrt_inv * moved, axis=0, keepdims=True)
    mean_weights = jnp.sum(sqrt_inv * half, axis=1, keepdims=True)
    transform = mean_weights + math.sqrt(members - 1.0) * sqrt_inv - eye
    flipped = transform.T
    high = flipped.astype(jnp.bfloat16)
    low = (flipped - high.astype(jnp.float32)).astype(jnp.bfloat16)
    left = jnp.concatenate([high, high, low, low], axis=1)

    rows_out = out_ref.reshape(members, 48, 128)
    leave = [
        pltpu.make_async_copy(
            rows_out.at[:, pl.ds(16 * i, 16), :], out.at[:, pl.ds(16 * i, 16), :], sems.at[i]
        )
        for i in range(3)
    ]

    def apply(pair_of, places_of):
        results = []
        for pair in pair_of:
            right = jnp.concatenate([pair, pair], axis=0)
            results.append(jnp.dot(left, right, preferred_element_type=jnp.float32))
        for result, rows in zip(results, places_of):
            for j in range(2):
                out_ref[pl.ds(rows[j], members, stride=48), :] = result[:, 128 * j : 128 * j + 128]

    for i in range(3):
        first = 2 * INNER * i
        pairs = [
            jnp.concatenate([dev_ref[first + 2 * k], dev_ref[first + 2 * k + 1]], axis=1)
            for k in range(INNER)
        ]
        pairs.append(jnp.concatenate([outer_ref[2 * i], outer_ref[2 * i + 1]], axis=1))
        spots = [[r + r // INNER + 1 for r in (first + 2 * k, first + 2 * k + 1)] for k in range(INNER)]
        spots.append([16 * i, 16 * i + 8])
        apply(pairs, spots)
        leave[i].start()
    for copy in leave:
        copy.wait()


def unpack_kernel(packed, land, out, field, sems):
    copies = [
        pltpu.make_async_copy(field.at[m, :, g], out.at[m, :, :, pl.ds(128 * g, 128)], sems.at[m, g])
        for m in range(4)
        for g in range(2)
    ]
    masks = {}
    for qx in range(2):
        for g in range(2):
            for a in range(4):
                rows = land[g, pl.ds(32 * qx + a, 8, stride=4), :]
                masks[qx, g, a] = rows
    for m in range(4):
        for i in range(0, len(BLOCKS), 12):
            todo = BLOCKS[i : i + 12]
            tiles = swap_blocks(
                [
                    [
                        packed[qx * 8 + g * 4 + b, 48 * m + 8 * f : 48 * m + 8 * f + 8, :]
                        for b in range(4)
                    ]
                    for f, qx, g in todo
                ]
            )
            for (f, qx, g), z in zip(todo, tiles):
                for a in range(4):
                    tile = pltpu.roll(z[a], 7, 0) if qx else z[a]
                    field[m, f, g, pl.ds(32 * qx + a, 8, stride=4), :] = tile * masks[qx, g, a]
        for g in range(2):
            copies[2 * m + g].start()
    for copy in copies:
        copy.wait()


def shape(*dims):
    return jax.ShapeDtypeStruct(dims, jnp.float32)


def local(initial_realizations, land_mask, obs_index, obs_count, obs_value, obs_error):
    whole = pl.BlockSpec(memory_space=pltpu.VMEM)
    far = pl.BlockSpec(memory_space=pltpu.HBM)
    to_high, to_low = pl.pallas_call(
        edges_kernel,
        out_shape=[shape(25, HALO, 256)] * 2,
        in_specs=[far, far],
        out_specs=[whole, whole],
        scratch_shapes=[
            pltpu.VMEM((4, 6, 8, 256), jnp.float32),
            pltpu.VMEM((4, 6, 8, 256), jnp.float32),
            pltpu.VMEM((8, 256), jnp.int32),
            pltpu.VMEM((8, 256), jnp.int32),
            pltpu.SemaphoreType.DMA((4,)),
        ],
        cost_estimate=pl.CostEstimate(flops=100000, bytes_accessed=800000, transcendentals=0),
    )(initial_realizations, land_mask)
    count = lax.axis_size("domain")
    forward = [(i, (i + 1) % count) for i in range(count)]
    backward = [(target, source) for source, target in forward]
    from_low = lax.ppermute(to_high, "domain", forward)
    from_high = lax.ppermute(to_low, "domain", backward)
    inner = pl.pallas_call(
        inner_kernel,
        out_shape=shape(16, 4 * INNER_ROWS, 128),
        in_specs=[far, far],
        out_specs=far,
        scratch_shapes=[
            pltpu.VMEM((4, 6, 64, 256), jnp.float32),
            pltpu.VMEM((64, 256), jnp.int32),
            pltpu.VMEM((16, 4 * INNER_ROWS, 128), jnp.float32),
            pltpu.VMEM((2, 6, 2, 64, 128), jnp.float32),
            pltpu.SemaphoreType.DMA((9,)),
        ],
        compiler_params=pltpu.CompilerParams(vmem_limit_bytes=WHOLE_VMEM),
        cost_estimate=pl.CostEstimate(flops=20000000, bytes_accessed=3000000, transcendentals=0),
    )(initial_realizations, land_mask)
    outer = pl.pallas_call(
        outer_kernel,
        out_shape=shape(16, 24, 128),
        in_specs=[whole] * 4,
        out_specs=whole,
        scratch_shapes=[pltpu.VMEM((2, 192, 128), jnp.float32)],
        compiler_params=pltpu.CompilerParams(vmem_limit_bytes=VMEM_LIMIT),
        cost_estimate=pl.CostEstimate(flops=10000000, bytes_accessed=3000000, transcendentals=0),
    )(initial_realizations, land_mask, from_low, from_high)
    inner = lax.all_to_all(inner, "member", split_axis=0, concat_axis=0, tiled=True)
    outer = lax.all_to_all(outer, "member", split_axis=0, concat_axis=0, tiled=True)
    observed, deviations = pl.pallas_call(
        gather_kernel,
        out_shape=[shape(64, 256), jax.ShapeDtypeStruct((INNER_ROWS, 128, 128), jnp.bfloat16)],
        in_specs=[whole] * 2,
        out_specs=[whole] * 2,
        compiler_params=pltpu.CompilerParams(vmem_limit_bytes=VMEM_LIMIT),
        cost_estimate=pl.CostEstimate(flops=10000000, bytes_accessed=3000000, transcendentals=0),
    )(inner.reshape(64 * INNER_ROWS, 128), obs_index[0])
    increment = pl.pallas_call(
        analysis_kernel,
        out_shape=shape(64, 48, 128),
        in_specs=[whole] * 7,
        out_specs=far,
        scratch_shapes=[
            pltpu.VMEM((3072, 128), jnp.float32),
            pltpu.VMEM((6, 128, 128), jnp.bfloat16),
            pltpu.SemaphoreType.DMA((3,)),
        ],
        compiler_params=pltpu.CompilerParams(vmem_limit_bytes=VMEM_LIMIT),
        cost_estimate=pl.CostEstimate(flops=60000000, bytes_accessed=3000000, transcendentals=0),
    )(
        outer.reshape(384, 128),
        observed,
        deviations,
        obs_index[0],
        obs_count,
        obs_value[0],
        obs_error[0],
    )
    returned = lax.all_to_all(
        increment.reshape(16, 192, 128), "member", split_axis=0, concat_axis=0, tiled=True
    )
    ocean = land_mask.astype(jnp.float32).reshape(64, 2, 128).transpose(1, 0, 2)
    return pl.pallas_call(
        unpack_kernel,
        out_shape=shape(4, 6, 64, 256),
        in_specs=[whole, whole],
        out_specs=far,
        scratch_shapes=[pltpu.VMEM((4, 6, 2, 64, 128), jnp.float32), pltpu.SemaphoreType.DMA((4, 2))],
        compiler_params=pltpu.CompilerParams(vmem_limit_bytes=VMEM_LIMIT),
    )(returned, ocean)


def solution(mesh):
    in_specs = (
        P("member", None, "domain", None),
        P("domain", None),
        P("domain", "member", None),
        P("domain", "member"),
        P("domain", "member", None),
        P("domain", "member", None),
    )
    out_specs = P("member", None, "domain", None)
    return jax.shard_map(local, mesh=mesh, in_specs=in_specs, out_specs=out_specs, check_vma=False)
```

```python
import math

import jax
import jax.numpy as jnp
from jax import lax
from jax.experimental import pallas as pl
from jax.experimental.pallas import tpu as pltpu
from jax.sharding import PartitionSpec as P

NS_ITERS = 8
CORIOLIS = 0.1
STRATIFY = 1.5
HALO = 4
SCAN = 14
VMEM_LIMIT = 48 * 1024 * 1024
WHOLE_VMEM = 62 * 1024 * 1024


def east(field):
    return tuple(pltpu.roll(x, x.shape[0] - 1, 0) - pltpu.roll(x, 1, 0) for x in field)


def north(field, first, last):
    west, rest = field
    west_up, rest_up = pltpu.roll(west, 1, 1), pltpu.roll(rest, 1, 1)
    west_down, rest_down = pltpu.roll(west, 127, 1), pltpu.roll(rest, 127, 1)
    return (
        jnp.where(last, rest_down, west_down) - jnp.where(first, 0.0, west_up),
        jnp.where(last, 0.0, rest_down) - jnp.where(first, west_up, rest_up),
    )


def step(state, mask, first, last):
    u1, v1, h1, u2, v2, h2 = state
    halves = range(2)
    du, dv = east(u1), north(v1, first, last)
    h1 = tuple(h1[i] - 0.125 * (du[i] + dv[i]) for i in halves)
    du, dv = east(u2), north(v2, first, last)
    h2 = tuple(h2[i] - 0.0625 * (du[i] + dv[i]) for i in halves)

    def turn(u, v, p):
        px, py = east(p), north(p, first, last)
        return (
            tuple((u[i] + CORIOLIS * v[i] - 0.125 * px[i]) * mask[i] for i in halves),
            tuple((v[i] - CORIOLIS * u[i] - 0.125 * py[i]) * mask[i] for i in halves),
        )

    u1, v1 = turn(u1, v1, tuple(h1[i] + h2[i] for i in halves))
    u2, v2 = turn(u2, v2, tuple(h1[i] + STRATIFY * h2[i] for i in halves))
    return (u1, v1, h1, u2, v2, h2)


def halves_of(x):
    return (x[..., 0:128], x[..., 128:256])


def forecast(state, mask):
    lane = lax.broadcasted_iota(jnp.int32, mask.shape[:1] + (128,), 1)
    first = lane == 0
    last = lane == 127
    state = tuple(halves_of(x) for x in state)
    mask = halves_of(mask)
    for _ in range(2):
        state = step(state, mask, first, last)
    return state


def skew(x, odd, high):
    once = [jnp.where(odd, x[(i + 1) % 4], x[i]) for i in range(4)]
    return [jnp.where(high, once[(i + 2) % 4], once[i]) for i in range(4)]


def swap_blocks(groups):
    lane = lax.broadcasted_iota(jnp.int32, (8, 128), 1)
    odd = (lane & 32) != 0
    high = lane >= 64
    skewed = [skew(x, odd, high) for x in groups]
    turned = [[w[0]] + [pltpu.roll(w[d], 32 * d, 1) for d in range(1, 4)] for w in skewed]
    back = [skew(w, odd, high) for w in turned]
    return [(w[0], w[3], w[2], w[1]) for w in back]


BLOCKS = [(f, qx, g) for f in range(6) for qx in range(2) for g in range(2)]
INNER = 7
INNER_ROWS = 6 * INNER


def edges_kernel(state, land, low_out, high_out, top, bottom, land_top, land_bottom, sems):
    copies = [
        pltpu.make_async_copy(state.at[:, :, 0:8, :], top, sems.at[0]),
        pltpu.make_async_copy(state.at[:, :, 56:64, :], bottom, sems.at[1]),
        pltpu.make_async_copy(land.at[0:8, :], land_top, sems.at[2]),
        pltpu.make_async_copy(land.at[56:64, :], land_bottom, sems.at[3]),
    ]
    for copy in copies:
        copy.start()
    for copy in copies:
        copy.wait()
    low_out[24] = land_bottom[8 - HALO :, :].astype(jnp.float32)
    high_out[24] = land_top[:HALO, :].astype(jnp.float32)
    for m in range(4):
        for f in range(6):
            low_out[6 * m + f] = bottom[m, f, 8 - HALO :, :]
            high_out[6 * m + f] = top[m, f, :HALO, :]


CUTS = (0, 40, 80, 120, 168)


def inner_kernel(state, land, out, begin, land_ref, packed, fields_ref, sems):
    arrive = [pltpu.make_async_copy(land, land_ref, sems.at[0])]
    arrive += [pltpu.make_async_copy(state.at[m], begin.at[m], sems.at[1 + m]) for m in range(4)]
    leave = [
        pltpu.make_async_copy(
            packed.at[:, pl.ds(CUTS[m], CUTS[m + 1] - CUTS[m]), :],
            out.at[:, pl.ds(CUTS[m], CUTS[m + 1] - CUTS[m]), :],
            sems.at[5 + m],
        )
        for m in range(4)
    ]
    for copy in arrive:
        copy.start()
    arrive[0].wait()
    mask = land_ref[...].astype(jnp.float32)
    for m in range(4):
        arrive[1 + m].wait()
        fields = forecast(tuple(begin[m, f] for f in range(6)), mask)
        for f in range(6):
            for g in range(2):
                fields_ref[m % 2, f, g] = fields[f][g]
        for i in range(0, len(BLOCKS), 12):
            todo = BLOCKS[i : i + 12]
            tiles = swap_blocks(
                [
                    [fields_ref[m % 2, f, g, pl.ds((4, 32)[qx] + a, 8, stride=4), :] for a in range(4)]
                    for f, qx, g in todo
                ]
            )
            for (f, qx, g), z in zip(todo, tiles):
                row = m * INNER_ROWS + f * INNER
                for b in range(4):
                    packed[qx * 8 + g * 4 + b, row : row + INNER, :] = z[b][0:INNER]
        leave[m].start()
    for copy in leave:
        copy.wait()


def outer_kernel(state, land, from_low, from_high, packed, fields_ref):
    mask = jnp.concatenate(
        [
            land[0:16, :].astype(jnp.float32),
            land[48:64, :].astype(jnp.float32),
            from_high[24],
            from_low[24],
        ],
        axis=0,
    )

    def one(m, carry):
        begin = tuple(
            jnp.concatenate(
                [state[m, f, 0:16, :], state[m, f, 48:64, :], from_high[6 * m + f], from_low[6 * m + f]],
                axis=0,
            )
            for f in range(6)
        )
        fields = forecast(begin, mask)
        for f in range(6):
            for g in range(2):
                sides = jnp.concatenate([fields[f][g][0:4], fields[f][g][28:32]], axis=0)
                fields_ref[g, pl.ds(pl.multiple_of((6 * m + f) * 8, 8), 8), :] = sides
        return carry

    lax.fori_loop(0, 4, one, 0)
    todo = [(i, qx, g) for i in range(3) for qx in range(2) for g in range(2)]
    tiles = swap_blocks(
        [
            [fields_ref[g, pl.ds(64 * i + 4 * qx + a, 8, stride=8), :] for a in range(4)]
            for i, qx, g in todo
        ]
    )
    for (i, qx, g), z in zip(todo, tiles):
        for b in range(4):
            packed[qx * 8 + g * 4 + b, 8 * i : 8 * i + 8, :] = z[b]


def places(index, members):
    chosen = index[...]
    side = lax.axis_index("member") // 8
    field = chosen >> 10
    group = ((chosen >> 7) + side) & 7
    row = jnp.where(group == 0, INNER_ROWS + field, field * INNER + group - 1)
    lane = chosen & 127
    halves = [slice(0, 128), slice(128, 256)]
    return (
        [jnp.broadcast_to(row[:, half], (members, 128)) for half in halves],
        [jnp.broadcast_to(lane[:, half], (members, 128)) for half in halves],
    )


def pick(tile, r, rows_of, lanes_of, acc):
    return tuple(
        jnp.where(rows_of[half] == r, jnp.take_along_axis(tile, lanes_of[half], axis=1), acc[half])
        for half in range(2)
    )


def split(x):
    members = x.shape[0]
    dev = x - jnp.sum(x, axis=0, keepdims=True) * (1.0 / members)
    high = dev.astype(jnp.bfloat16)
    return high, (dev - high.astype(jnp.float32)).astype(jnp.bfloat16)


def gather_kernel(x_ref, index, observed, dev_ref):
    members = 64
    rows_of, lanes_of = places(index, members)

    def scan(block, acc):
        rows = [block * SCAN + i for i in range(SCAN)]
        tiles = [x_ref[pl.ds(r, members, stride=INNER_ROWS), :] for r in rows]
        for r, tile in zip(rows, tiles):
            acc = pick(tile, r, rows_of, lanes_of, acc)
        for r, tile in zip(rows, tiles):
            high, low = split(tile)
            dev_ref[r, 0:members, :] = high
            dev_ref[r, members:, :] = low
        return acc

    zero = jnp.zeros((members, 128), jnp.float32)
    acc = lax.fori_loop(0, INNER_ROWS // SCAN, scan, (zero, zero))
    observed[:, 0:128] = acc[0]
    observed[:, 128:256] = acc[1]


def analysis_kernel(
    x_ref, picked, dev_ref, index, count, values, errors, out, out_ref, outer_ref, sems
):
    members = 64
    rows_of, lanes_of = places(index, members)
    acc = (picked[:, 0:128], picked[:, 128:256])
    for f in range(6):
        tile = x_ref[pl.ds(f, members, stride=6), :]
        acc = pick(tile, INNER_ROWS + f, rows_of, lanes_of, acc)
        high, low = split(tile)
        outer_ref[f, 0:members, :] = high
        outer_ref[f, members:, :] = low
    observed = jnp.concatenate(acc, axis=1)
    obs_mean = jnp.sum(observed, axis=0, keepdims=True) * (1.0 / members)
    spread = observed - obs_mean
    slots = lax.broadcasted_iota(jnp.int32, (1, 256), 1)
    weight = jnp.where(slots < count[...], 1.0 / errors[...], 0.0)
    innovation = values[...] - obs_mean
    scaled = spread * weight
    eye = (
        lax.broadcasted_iota(jnp.int32, (members, members), 0)
        == lax.broadcasted_iota(jnp.int32, (members, members), 1)
    ).astype(jnp.float32)

    def parts(a):
        high = a.astype(jnp.bfloat16)
        return high, (a - high.astype(jnp.float32)).astype(jnp.bfloat16)

    def times(a, b):
        left = jnp.concatenate(a, axis=1)
        right = jnp.concatenate(b + b, axis=0)
        return jnp.dot(left, right, preferred_element_type=jnp.float32)

    scaled_high, scaled_low = parts(scaled)
    spread_high, spread_low = parts(spread)

    def over_slots(a, b):
        return lax.dot_general(a, b, (((1,), (1,)), ((), ())), preferred_element_type=jnp.float32)

    gram = over_slots(scaled_high, spread_high) + (
        over_slots(scaled_high, spread_low) + over_slots(scaled_low, spread_high)
    )
    moved = jnp.sum(eye * jnp.sum(scaled * innovation, axis=1, keepdims=True), axis=0, keepdims=True)
    system = (members - 1.0) * eye + gram
    total = jnp.sum(jnp.sum(system * system, axis=1, keepdims=True), axis=0, keepdims=True)
    norm = jnp.sqrt(total)
    twice = jnp.concatenate([eye, eye], axis=1)
    root = jnp.concatenate([system, system], axis=1) / norm
    inverse = twice
    for sweep in range(NS_ITERS):
        root_parts, inverse_parts = parts(root), parts(inverse)
        factor = 1.5 * twice - 0.5 * (root if sweep == 0 else times(inverse_parts, root_parts))
        factor_parts = parts(factor)
        if sweep < NS_ITERS - 1:
            root = times(root_parts, factor_parts)
        inverse = factor if sweep == 0 else times(factor_parts, inverse_parts)
    sqrt_inv = inverse[:, 0:members] / jnp.sqrt(norm)
    half = jnp.sum(sqrt_inv * moved, axis=1, keepdims=True)
    mean_weights = jnp.sum(sqrt_inv * half, axis=0, keepdims=True)
    flipped = mean_weights + math.sqrt(members - 1.0) * sqrt_inv - eye
    high = flipped.astype(jnp.bfloat16)
    low = (flipped - high.astype(jnp.float32)).astype(jnp.bfloat16)
    left = jnp.concatenate([high, high, low, low], axis=1)

    rows_out = out_ref.reshape(members, 48, 128)
    leave = [
        pltpu.make_async_copy(
            rows_out.at[:, pl.ds(16 * i, 16), :], out.at[:, pl.ds(16 * i, 16), :], sems.at[i]
        )
        for i in range(3)
    ]

    def apply(pair_of, places_of):
        results = []
        for pair in pair_of:
            right = jnp.concatenate([pair, pair], axis=0)
            results.append(jnp.dot(left, right, preferred_element_type=jnp.float32))
        for result, rows in zip(results, places_of):
            for j in range(2):
                out_ref[pl.ds(rows[j], members, stride=48), :] = result[:, 128 * j : 128 * j + 128]

    for i in range(3):
        first = 2 * INNER * i
        pairs = [
            jnp.concatenate([dev_ref[first + 2 * k], dev_ref[first + 2 * k + 1]], axis=1)
            for k in range(INNER)
        ]
        pairs.append(jnp.concatenate([outer_ref[2 * i], outer_ref[2 * i + 1]], axis=1))
        spots = [[r + r // INNER + 1 for r in (first + 2 * k, first + 2 * k + 1)] for k in range(INNER)]
        spots.append([16 * i, 16 * i + 8])
        apply(pairs, spots)
        leave[i].start()
    for copy in leave:
        copy.wait()


def unpack_kernel(packed, land, out, field, sems):
    copies = [
        pltpu.make_async_copy(field.at[m, :, g], out.at[m, :, :, pl.ds(128 * g, 128)], sems.at[m, g])
        for m in range(4)
        for g in range(2)
    ]
    masks = {}
    for qx in range(2):
        for g in range(2):
            for a in range(4):
                rows = land[g, pl.ds(32 * qx + a, 8, stride=4), :]
                masks[qx, g, a] = rows
    for m in range(4):
        for i in range(0, len(BLOCKS), 12):
            todo = BLOCKS[i : i + 12]
            tiles = swap_blocks(
                [
                    [
                        packed[qx * 8 + g * 4 + b, 48 * m + 8 * f : 48 * m + 8 * f + 8, :]
                        for b in range(4)
                    ]
                    for f, qx, g in todo
                ]
            )
            for (f, qx, g), z in zip(todo, tiles):
                for a in range(4):
                    tile = pltpu.roll(z[a], 7, 0) if qx else z[a]
                    field[m, f, g, pl.ds(32 * qx + a, 8, stride=4), :] = tile * masks[qx, g, a]
        for g in range(2):
            copies[2 * m + g].start()
    for copy in copies:
        copy.wait()


def shape(*dims):
    return jax.ShapeDtypeStruct(dims, jnp.float32)


def local(initial_realizations, land_mask, obs_index, obs_count, obs_value, obs_error):
    whole = pl.BlockSpec(memory_space=pltpu.VMEM)
    far = pl.BlockSpec(memory_space=pltpu.HBM)
    to_high, to_low = pl.pallas_call(
        edges_kernel,
        out_shape=[shape(25, HALO, 256)] * 2,
        in_specs=[far, far],
        out_specs=[whole, whole],
        scratch_shapes=[
            pltpu.VMEM((4, 6, 8, 256), jnp.float32),
            pltpu.VMEM((4, 6, 8, 256), jnp.float32),
            pltpu.VMEM((8, 256), jnp.int32),
            pltpu.VMEM((8, 256), jnp.int32),
            pltpu.SemaphoreType.DMA((4,)),
        ],
        cost_estimate=pl.CostEstimate(flops=100000, bytes_accessed=800000, transcendentals=0),
    )(initial_realizations, land_mask)
    count = lax.axis_size("domain")
    forward = [(i, (i + 1) % count) for i in range(count)]
    backward = [(target, source) for source, target in forward]
    from_low = lax.ppermute(to_high, "domain", forward)
    from_high = lax.ppermute(to_low, "domain", backward)
    inner = pl.pallas_call(
        inner_kernel,
        out_shape=shape(16, 4 * INNER_ROWS, 128),
        in_specs=[far, far],
        out_specs=far,
        scratch_shapes=[
            pltpu.VMEM((4, 6, 64, 256), jnp.float32),
            pltpu.VMEM((64, 256), jnp.int32),
            pltpu.VMEM((16, 4 * INNER_ROWS, 128), jnp.float32),
            pltpu.VMEM((2, 6, 2, 64, 128), jnp.float32),
            pltpu.SemaphoreType.DMA((9,)),
        ],
        compiler_params=pltpu.CompilerParams(vmem_limit_bytes=WHOLE_VMEM),
        cost_estimate=pl.CostEstimate(flops=20000000, bytes_accessed=3000000, transcendentals=0),
    )(initial_realizations, land_mask)
    outer = pl.pallas_call(
        outer_kernel,
        out_shape=shape(16, 24, 128),
        in_specs=[whole] * 4,
        out_specs=whole,
        scratch_shapes=[pltpu.VMEM((2, 192, 128), jnp.float32)],
        compiler_params=pltpu.CompilerParams(vmem_limit_bytes=VMEM_LIMIT),
        cost_estimate=pl.CostEstimate(flops=10000000, bytes_accessed=3000000, transcendentals=0),
    )(initial_realizations, land_mask, from_low, from_high)
    inner = lax.all_to_all(inner, "member", split_axis=0, concat_axis=0, tiled=True)
    outer = lax.all_to_all(outer, "member", split_axis=0, concat_axis=0, tiled=True)
    observed, deviations = pl.pallas_call(
        gather_kernel,
        out_shape=[shape(64, 256), jax.ShapeDtypeStruct((INNER_ROWS, 128, 128), jnp.bfloat16)],
        in_specs=[whole] * 2,
        out_specs=[whole] * 2,
        compiler_params=pltpu.CompilerParams(vmem_limit_bytes=VMEM_LIMIT),
        cost_estimate=pl.CostEstimate(flops=10000000, bytes_accessed=3000000, transcendentals=0),
    )(inner.reshape(64 * INNER_ROWS, 128), obs_index[0])
    increment = pl.pallas_call(
        analysis_kernel,
        out_shape=shape(64, 48, 128),
        in_specs=[whole] * 7,
        out_specs=far,
        scratch_shapes=[
            pltpu.VMEM((3072, 128), jnp.float32),
            pltpu.VMEM((6, 128, 128), jnp.bfloat16),
            pltpu.SemaphoreType.DMA((3,)),
        ],
        compiler_params=pltpu.CompilerParams(vmem_limit_bytes=VMEM_LIMIT),
        cost_estimate=pl.CostEstimate(flops=60000000, bytes_accessed=3000000, transcendentals=0),
    )(
        outer.reshape(384, 128),
        observed,
        deviations,
        obs_index[0],
        obs_count,
        obs_value[0],
        obs_error[0],
    )
    returned = lax.all_to_all(
        increment.reshape(16, 192, 128), "member", split_axis=0, concat_axis=0, tiled=True
    )
    ocean = land_mask.astype(jnp.float32).reshape(64, 2, 128).transpose(1, 0, 2)
    return pl.pallas_call(
        unpack_kernel,
        out_shape=shape(4, 6, 64, 256),
        in_specs=[whole, whole],
        out_specs=far,
        scratch_shapes=[pltpu.VMEM((4, 6, 2, 64, 128), jnp.float32), pltpu.SemaphoreType.DMA((4, 2))],
        compiler_params=pltpu.CompilerParams(vmem_limit_bytes=VMEM_LIMIT),
    )(returned, ocean)


def solution(mesh):
    in_specs = (
        P("member", None, "domain", None),
        P("domain", None),
        P("domain", "member", None),
        P("domain", "member"),
        P("domain", "member", None),
        P("domain", "member", None),
    )
    out_specs = P("member", None, "domain", None)
    return jax.shard_map(local, mesh=mesh, in_specs=in_specs, out_specs=out_specs, check_vma=False)
```

```python
import math

import jax
import jax.numpy as jnp
from jax import lax
from jax.experimental import pallas as pl
from jax.experimental.pallas import tpu as pltpu
from jax.sharding import PartitionSpec as P

NS_ITERS = 8
CORIOLIS = 0.1
STRATIFY = 1.5
HALO = 4
SCAN = 14
VMEM_LIMIT = 48 * 1024 * 1024
WHOLE_VMEM = 62 * 1024 * 1024


def east(field):
    return tuple(pltpu.roll(x, x.shape[0] - 1, 0) - pltpu.roll(x, 1, 0) for x in field)


def north(field, first, last):
    west, rest = field
    west_up, rest_up = pltpu.roll(west, 1, 1), pltpu.roll(rest, 1, 1)
    west_down, rest_down = pltpu.roll(west, 127, 1), pltpu.roll(rest, 127, 1)
    return (
        jnp.where(last, rest_down, west_down) - jnp.where(first, 0.0, west_up),
        jnp.where(last, 0.0, rest_down) - jnp.where(first, west_up, rest_up),
    )


def step(state, mask, first, last):
    u1, v1, h1, u2, v2, h2 = state
    halves = range(2)
    du, dv = east(u1), north(v1, first, last)
    h1 = tuple(h1[i] - 0.125 * (du[i] + dv[i]) for i in halves)
    du, dv = east(u2), north(v2, first, last)
    h2 = tuple(h2[i] - 0.0625 * (du[i] + dv[i]) for i in halves)

    def turn(u, v, p):
        px, py = east(p), north(p, first, last)
        return (
            tuple((u[i] + CORIOLIS * v[i] - 0.125 * px[i]) * mask[i] for i in halves),
            tuple((v[i] - CORIOLIS * u[i] - 0.125 * py[i]) * mask[i] for i in halves),
        )

    u1, v1 = turn(u1, v1, tuple(h1[i] + h2[i] for i in halves))
    u2, v2 = turn(u2, v2, tuple(h1[i] + STRATIFY * h2[i] for i in halves))
    return (u1, v1, h1, u2, v2, h2)


def halves_of(x):
    return (x[..., 0:128], x[..., 128:256])


def forecast(state, mask):
    lane = lax.broadcasted_iota(jnp.int32, mask.shape[:1] + (128,), 1)
    first = lane == 0
    last = lane == 127
    state = tuple(halves_of(x) for x in state)
    mask = halves_of(mask)
    for _ in range(2):
        state = step(state, mask, first, last)
    return state


def skew(x, odd, high):
    once = [jnp.where(odd, x[(i + 1) % 4], x[i]) for i in range(4)]
    return [jnp.where(high, once[(i + 2) % 4], once[i]) for i in range(4)]


def swap_blocks(groups):
    lane = lax.broadcasted_iota(jnp.int32, (8, 128), 1)
    odd = (lane & 32) != 0
    high = lane >= 64
    skewed = [skew(x, odd, high) for x in groups]
    turned = [[w[0]] + [pltpu.roll(w[d], 32 * d, 1) for d in range(1, 4)] for w in skewed]
    back = [skew(w, odd, high) for w in turned]
    return [(w[0], w[3], w[2], w[1]) for w in back]


BLOCKS = [(f, qx, g) for f in range(6) for qx in range(2) for g in range(2)]
INNER = 7
INNER_ROWS = 6 * INNER


def edges_kernel(state, land, low_out, high_out, top, bottom, land_top, land_bottom, sems):
    copies = [
        pltpu.make_async_copy(state.at[:, :, 0:8, :], top, sems.at[0]),
        pltpu.make_async_copy(state.at[:, :, 56:64, :], bottom, sems.at[1]),
        pltpu.make_async_copy(land.at[0:8, :], land_top, sems.at[2]),
        pltpu.make_async_copy(land.at[56:64, :], land_bottom, sems.at[3]),
    ]
    for copy in copies:
        copy.start()
    for copy in copies:
        copy.wait()
    low_out[24] = land_bottom[8 - HALO :, :].astype(jnp.float32)
    high_out[24] = land_top[:HALO, :].astype(jnp.float32)
    for m in range(4):
        for f in range(6):
            low_out[6 * m + f] = bottom[m, f, 8 - HALO :, :]
            high_out[6 * m + f] = top[m, f, :HALO, :]


CUTS = (0, 40, 80, 120, 168)


def inner_kernel(state, land, out, begin, land_ref, packed, fields_ref, sems):
    arrive = [pltpu.make_async_copy(land, land_ref, sems.at[0])]
    arrive += [pltpu.make_async_copy(state.at[m], begin.at[m], sems.at[1 + m]) for m in range(4)]
    leave = [
        pltpu.make_async_copy(
            packed.at[:, pl.ds(CUTS[m], CUTS[m + 1] - CUTS[m]), :],
            out.at[:, pl.ds(CUTS[m], CUTS[m + 1] - CUTS[m]), :],
            sems.at[5 + m],
        )
        for m in range(4)
    ]
    for copy in arrive:
        copy.start()
    arrive[0].wait()
    mask = land_ref[...].astype(jnp.float32)
    mask = jnp.concatenate([mask, mask], axis=0)
    for pair in range(2):
        members = (2 * pair, 2 * pair + 1)
        for m in members:
            arrive[1 + m].wait()
        fields = forecast(
            tuple(jnp.concatenate([begin[m, f] for m in members], axis=0) for f in range(6)), mask
        )
        for m in members:
            for f in range(6):
                for g in range(2):
                    fields_ref[m % 2, f, g] = fields[f][g][64 * (m % 2) : 64 * (m % 2) + 64]
        for m in members:
            for i in range(0, len(BLOCKS), 12):
                todo = BLOCKS[i : i + 12]
                tiles = swap_blocks(
                    [
                        [
                            fields_ref[m % 2, f, g, pl.ds((4, 32)[qx] + a, 8, stride=4), :]
                            for a in range(4)
                        ]
                        for f, qx, g in todo
                    ]
                )
                for (f, qx, g), z in zip(todo, tiles):
                    row = m * INNER_ROWS + f * INNER
                    for b in range(4):
                        packed[qx * 8 + g * 4 + b, row : row + INNER, :] = z[b][0:INNER]
            leave[m].start()
    for copy in leave:
        copy.wait()


def outer_kernel(state, land, from_low, from_high, packed, fields_ref):
    mask = jnp.concatenate(
        [
            land[0:16, :].astype(jnp.float32),
            land[48:64, :].astype(jnp.float32),
            from_high[24],
            from_low[24],
        ],
        axis=0,
    )

    def one(m, carry):
        begin = tuple(
            jnp.concatenate(
                [state[m, f, 0:16, :], state[m, f, 48:64, :], from_high[6 * m + f], from_low[6 * m + f]],
                axis=0,
            )
            for f in range(6)
        )
        fields = forecast(begin, mask)
        for f in range(6):
            for g in range(2):
                sides = jnp.concatenate([fields[f][g][0:4], fields[f][g][28:32]], axis=0)
                fields_ref[g, pl.ds(pl.multiple_of((6 * m + f) * 8, 8), 8), :] = sides
        return carry

    lax.fori_loop(0, 4, one, 0)
    todo = [(i, qx, g) for i in range(3) for qx in range(2) for g in range(2)]
    tiles = swap_blocks(
        [
            [fields_ref[g, pl.ds(64 * i + 4 * qx + a, 8, stride=8), :] for a in range(4)]
            for i, qx, g in todo
        ]
    )
    for (i, qx, g), z in zip(todo, tiles):
        for b in range(4):
            packed[qx * 8 + g * 4 + b, 8 * i : 8 * i + 8, :] = z[b]


def places(index, members):
    chosen = index[...]
    side = lax.axis_index("member") // 8
    field = chosen >> 10
    group = ((chosen >> 7) + side) & 7
    row = jnp.where(group == 0, INNER_ROWS + field, field * INNER + group - 1)
    lane = chosen & 127
    halves = [slice(0, 128), slice(128, 256)]
    return (
        [jnp.broadcast_to(row[:, half], (members, 128)) for half in halves],
        [jnp.broadcast_to(lane[:, half], (members, 128)) for half in halves],
    )


def pick(tile, r, rows_of, lanes_of, acc):
    return tuple(
        jnp.where(rows_of[half] == r, jnp.take_along_axis(tile, lanes_of[half], axis=1), acc[half])
        for half in range(2)
    )


def split(x):
    members = x.shape[0]
    dev = x - jnp.sum(x, axis=0, keepdims=True) * (1.0 / members)
    high = dev.astype(jnp.bfloat16)
    return high, (dev - high.astype(jnp.float32)).astype(jnp.bfloat16)


def gather_kernel(x_ref, index, observed, dev_ref):
    members = 64
    rows_of, lanes_of = places(index, members)

    def scan(block, acc):
        rows = [block * SCAN + i for i in range(SCAN)]
        tiles = [x_ref[pl.ds(r, members, stride=INNER_ROWS), :] for r in rows]
        for r, tile in zip(rows, tiles):
            acc = pick(tile, r, rows_of, lanes_of, acc)
        for r, tile in zip(rows, tiles):
            high, low = split(tile)
            dev_ref[r, 0:members, :] = high
            dev_ref[r, members:, :] = low
        return acc

    zero = jnp.zeros((members, 128), jnp.float32)
    acc = lax.fori_loop(0, INNER_ROWS // SCAN, scan, (zero, zero))
    observed[:, 0:128] = acc[0]
    observed[:, 128:256] = acc[1]


def analysis_kernel(
    x_ref, picked, dev_ref, index, count, values, errors, out, out_ref, outer_ref, sems
):
    members = 64
    rows_of, lanes_of = places(index, members)
    acc = (picked[:, 0:128], picked[:, 128:256])
    for f in range(6):
        tile = x_ref[pl.ds(f, members, stride=6), :]
        acc = pick(tile, INNER_ROWS + f, rows_of, lanes_of, acc)
        high, low = split(tile)
        outer_ref[f, 0:members, :] = high
        outer_ref[f, members:, :] = low
    observed = jnp.concatenate(acc, axis=1)
    obs_mean = jnp.sum(observed, axis=0, keepdims=True) * (1.0 / members)
    spread = observed - obs_mean
    slots = lax.broadcasted_iota(jnp.int32, (1, 256), 1)
    weight = jnp.where(slots < count[...], 1.0 / errors[...], 0.0)
    innovation = values[...] - obs_mean
    scaled = spread * weight
    column = lax.broadcasted_iota(jnp.int32, (members, 2 * members), 1)
    line = lax.broadcasted_iota(jnp.int32, (members, 2 * members), 0)
    twice = (line == (column & (members - 1))).astype(jnp.float32)
    once = (line == column).astype(jnp.float32)

    def parts(a, count=3):
        found = []
        for _ in range(count):
            found.append(a.astype(jnp.bfloat16))
            a = a - found[-1].astype(jnp.float32)
        return found

    nothing = jnp.zeros((members, 2 * members), jnp.bfloat16)

    def times(a, b):
        (ah, am, al), (bh, bm, bl) = a, b
        coarse = jnp.dot(
            jnp.concatenate([ah, am], axis=1),
            jnp.concatenate([bh, bm, bh, bm], axis=0),
            preferred_element_type=jnp.float32,
        )
        fine = jnp.dot(
            jnp.concatenate([al, ah], axis=1),
            jnp.concatenate([bh, bm, bl, nothing], axis=0),
            preferred_element_type=jnp.float32,
        )
        return coarse + fine

    def over_slots(a, b):
        return lax.dot_general(
            a,
            jnp.concatenate([b, b], axis=0),
            (((1,), (1,)), ((), ())),
            preferred_element_type=jnp.float32,
        )

    (ah, am, al), (bh, bm, bl) = parts(scaled), parts(spread)
    gram = over_slots(ah, bh) + (
        (over_slots(ah, bm) + over_slots(am, bh))
        + (over_slots(am, bm) + over_slots(ah, bl) + over_slots(al, bh))
    )
    moved = jnp.sum(once * jnp.sum(scaled * innovation, axis=1, keepdims=True), axis=0, keepdims=True)
    system = (members - 1.0) * twice + gram
    system_parts = parts(system)
    square = times(system_parts, system_parts)
    total = 0.5 * jnp.sum(jnp.sum(system * system, axis=0, keepdims=True), axis=1, keepdims=True)
    norm_inv = lax.rsqrt(total)
    norm_inv_root = jnp.sqrt(norm_inv)
    root = system * norm_inv
    inverse = 1.5 * twice - 0.5 * root
    root = 1.5 * root - 0.5 * (square * norm_inv * norm_inv)
    for sweep in range(1, NS_ITERS):
        root_parts, inverse_parts = parts(root), parts(inverse)
        factor = 1.5 * twice - 0.5 * times(inverse_parts, root_parts)
        factor_parts = parts(factor)
        if sweep < NS_ITERS - 1:
            root = times(root_parts, factor_parts)
            inverse = times(factor_parts, inverse_parts)
    left_half = (column[0:1] < members).astype(jnp.float32)
    weights = moved
    for _ in range(2):
        step_one = jnp.sum(inverse * weights, axis=1, keepdims=True)
        weights = jnp.sum(factor * step_one, axis=0, keepdims=True) * left_half
    weights = weights + pltpu.roll(weights, members, 1)
    sqrt_inv = times(factor_parts, inverse_parts) * norm_inv_root
    flipped = weights * norm_inv + math.sqrt(members - 1.0) * sqrt_inv - twice
    left = jnp.concatenate(parts(flipped, 2), axis=1)

    rows_out = out_ref.reshape(members, 48, 128)
    leave = [
        pltpu.make_async_copy(
            rows_out.at[:, pl.ds(16 * i, 16), :], out.at[:, pl.ds(16 * i, 16), :], sems.at[i]
        )
        for i in range(3)
    ]

    def apply(pair_of, places_of):
        results = []
        for pair in pair_of:
            right = jnp.concatenate([pair, pair], axis=0)
            results.append(jnp.dot(left, right, preferred_element_type=jnp.float32))
        for result, rows in zip(results, places_of):
            for j in range(2):
                out_ref[pl.ds(rows[j], members, stride=48), :] = result[:, 128 * j : 128 * j + 128]

    for i in range(3):
        first = 2 * INNER * i
        pairs = [
            jnp.concatenate([dev_ref[first + 2 * k], dev_ref[first + 2 * k + 1]], axis=1)
            for k in range(INNER)
        ]
        pairs.append(jnp.concatenate([outer_ref[2 * i], outer_ref[2 * i + 1]], axis=1))
        spots = [[r + r // INNER + 1 for r in (first + 2 * k, first + 2 * k + 1)] for k in range(INNER)]
        spots.append([16 * i, 16 * i + 8])
        apply(pairs, spots)
        leave[i].start()
    for copy in leave:
        copy.wait()


def unpack_kernel(packed, land, out, field, sems):
    copies = [
        pltpu.make_async_copy(field.at[m, :, g], out.at[m, :, :, pl.ds(128 * g, 128)], sems.at[m, g])
        for m in range(4)
        for g in range(2)
    ]
    masks = {}
    for qx in range(2):
        for g in range(2):
            for a in range(4):
                rows = land[g, pl.ds(32 * qx + a, 8, stride=4), :]
                masks[qx, g, a] = rows
    for m in range(4):
        for i in range(0, len(BLOCKS), 12):
            todo = BLOCKS[i : i + 12]
            tiles = swap_blocks(
                [
                    [
                        packed[qx * 8 + g * 4 + b, 48 * m + 8 * f : 48 * m + 8 * f + 8, :]
                        for b in range(4)
                    ]
                    for f, qx, g in todo
                ]
            )
            for (f, qx, g), z in zip(todo, tiles):
                for a in range(4):
                    tile = pltpu.roll(z[a], 7, 0) if qx else z[a]
                    field[m, f, g, pl.ds(32 * qx + a, 8, stride=4), :] = tile * masks[qx, g, a]
        for g in range(2):
            copies[2 * m + g].start()
    for copy in copies:
        copy.wait()


def shape(*dims):
    return jax.ShapeDtypeStruct(dims, jnp.float32)


def local(initial_realizations, land_mask, obs_index, obs_count, obs_value, obs_error):
    whole = pl.BlockSpec(memory_space=pltpu.VMEM)
    far = pl.BlockSpec(memory_space=pltpu.HBM)
    to_high, to_low = pl.pallas_call(
        edges_kernel,
        out_shape=[shape(25, HALO, 256)] * 2,
        in_specs=[far, far],
        out_specs=[whole, whole],
        scratch_shapes=[
            pltpu.VMEM((4, 6, 8, 256), jnp.float32),
            pltpu.VMEM((4, 6, 8, 256), jnp.float32),
            pltpu.VMEM((8, 256), jnp.int32),
            pltpu.VMEM((8, 256), jnp.int32),
            pltpu.SemaphoreType.DMA((4,)),
        ],
        cost_estimate=pl.CostEstimate(flops=100000, bytes_accessed=800000, transcendentals=0),
    )(initial_realizations, land_mask)
    count = lax.axis_size("domain")
    forward = [(i, (i + 1) % count) for i in range(count)]
    backward = [(target, source) for source, target in forward]
    from_low = lax.ppermute(to_high, "domain", forward)
    from_high = lax.ppermute(to_low, "domain", backward)
    inner = pl.pallas_call(
        inner_kernel,
        out_shape=shape(16, 4 * INNER_ROWS, 128),
        in_specs=[far, far],
        out_specs=far,
        scratch_shapes=[
            pltpu.VMEM((4, 6, 64, 256), jnp.float32),
            pltpu.VMEM((64, 256), jnp.int32),
            pltpu.VMEM((16, 4 * INNER_ROWS, 128), jnp.float32),
            pltpu.VMEM((2, 6, 2, 64, 128), jnp.float32),
            pltpu.SemaphoreType.DMA((9,)),
        ],
        compiler_params=pltpu.CompilerParams(vmem_limit_bytes=WHOLE_VMEM),
        cost_estimate=pl.CostEstimate(flops=20000000, bytes_accessed=3000000, transcendentals=0),
    )(initial_realizations, land_mask)
    outer = pl.pallas_call(
        outer_kernel,
        out_shape=shape(16, 24, 128),
        in_specs=[whole] * 4,
        out_specs=whole,
        scratch_shapes=[pltpu.VMEM((2, 192, 128), jnp.float32)],
        compiler_params=pltpu.CompilerParams(vmem_limit_bytes=VMEM_LIMIT),
        cost_estimate=pl.CostEstimate(flops=10000000, bytes_accessed=3000000, transcendentals=0),
    )(initial_realizations, land_mask, from_low, from_high)
    inner = lax.all_to_all(inner, "member", split_axis=0, concat_axis=0, tiled=True)
    outer = lax.all_to_all(outer, "member", split_axis=0, concat_axis=0, tiled=True)
    observed, deviations = pl.pallas_call(
        gather_kernel,
        out_shape=[shape(64, 256), jax.ShapeDtypeStruct((INNER_ROWS, 128, 128), jnp.bfloat16)],
        in_specs=[whole] * 2,
        out_specs=[whole] * 2,
        compiler_params=pltpu.CompilerParams(vmem_limit_bytes=VMEM_LIMIT),
        cost_estimate=pl.CostEstimate(flops=10000000, bytes_accessed=3000000, transcendentals=0),
    )(inner.reshape(64 * INNER_ROWS, 128), obs_index[0])
    increment = pl.pallas_call(
        analysis_kernel,
        out_shape=shape(64, 48, 128),
        in_specs=[whole] * 7,
        out_specs=far,
        scratch_shapes=[
            pltpu.VMEM((3072, 128), jnp.float32),
            pltpu.VMEM((6, 128, 128), jnp.bfloat16),
            pltpu.SemaphoreType.DMA((3,)),
        ],
        compiler_params=pltpu.CompilerParams(vmem_limit_bytes=VMEM_LIMIT),
        cost_estimate=pl.CostEstimate(flops=60000000, bytes_accessed=3000000, transcendentals=0),
    )(
        outer.reshape(384, 128),
        observed,
        deviations,
        obs_index[0],
        obs_count,
        obs_value[0],
        obs_error[0],
    )
    returned = lax.all_to_all(
        increment.reshape(16, 192, 128), "member", split_axis=0, concat_axis=0, tiled=True
    )
    ocean = land_mask.astype(jnp.float32).reshape(64, 2, 128).transpose(1, 0, 2)
    return pl.pallas_call(
        unpack_kernel,
        out_shape=shape(4, 6, 64, 256),
        in_specs=[whole, whole],
        out_specs=far,
        scratch_shapes=[pltpu.VMEM((4, 6, 2, 64, 128), jnp.float32), pltpu.SemaphoreType.DMA((4, 2))],
        compiler_params=pltpu.CompilerParams(vmem_limit_bytes=VMEM_LIMIT),
    )(returned, ocean)


def solution(mesh):
    in_specs = (
        P("member", None, "domain", None),
        P("domain", None),
        P("domain", "member", None),
        P("domain", "member"),
        P("domain", "member", None),
        P("domain", "member", None),
    )
    out_specs = P("member", None, "domain", None)
    return jax.shard_map(local, mesh=mesh, in_specs=in_specs, out_specs=out_specs, check_vma=False)
```

```python
import math

import jax
import jax.numpy as jnp
from jax import lax
from jax.experimental import pallas as pl
from jax.experimental.pallas import tpu as pltpu
from jax.sharding import PartitionSpec as P

NS_ITERS = 8
CORIOLIS = 0.1
STRATIFY = 1.5
HALO = 4
SCAN = 14
VMEM_LIMIT = 48 * 1024 * 1024
WHOLE_VMEM = 62 * 1024 * 1024


def east(field):
    return tuple(pltpu.roll(x, x.shape[0] - 1, 0) - pltpu.roll(x, 1, 0) for x in field)


def north(field, first, last):
    west, rest = field
    west_up, rest_up = pltpu.roll(west, 1, 1), pltpu.roll(rest, 1, 1)
    west_down, rest_down = pltpu.roll(west, 127, 1), pltpu.roll(rest, 127, 1)
    return (
        jnp.where(last, rest_down, west_down) - jnp.where(first, 0.0, west_up),
        jnp.where(last, 0.0, rest_down) - jnp.where(first, west_up, rest_up),
    )


def step(state, mask, first, last):
    u1, v1, h1, u2, v2, h2 = state
    halves = range(2)
    du, dv = east(u1), north(v1, first, last)
    h1 = tuple(h1[i] - 0.125 * (du[i] + dv[i]) for i in halves)
    du, dv = east(u2), north(v2, first, last)
    h2 = tuple(h2[i] - 0.0625 * (du[i] + dv[i]) for i in halves)

    def turn(u, v, p):
        px, py = east(p), north(p, first, last)
        return (
            tuple((u[i] + CORIOLIS * v[i] - 0.125 * px[i]) * mask[i] for i in halves),
            tuple((v[i] - CORIOLIS * u[i] - 0.125 * py[i]) * mask[i] for i in halves),
        )

    u1, v1 = turn(u1, v1, tuple(h1[i] + h2[i] for i in halves))
    u2, v2 = turn(u2, v2, tuple(h1[i] + STRATIFY * h2[i] for i in halves))
    return (u1, v1, h1, u2, v2, h2)


def halves_of(x):
    return (x[..., 0:128], x[..., 128:256])


def forecast(state, mask):
    lane = lax.broadcasted_iota(jnp.int32, mask.shape[:1] + (128,), 1)
    first = lane == 0
    last = lane == 127
    state = tuple(halves_of(x) for x in state)
    mask = halves_of(mask)
    for _ in range(2):
        state = step(state, mask, first, last)
    return state


def skew(x, odd, high):
    once = [jnp.where(odd, x[(i + 1) % 4], x[i]) for i in range(4)]
    return [jnp.where(high, once[(i + 2) % 4], once[i]) for i in range(4)]


def swap_blocks(groups):
    lane = lax.broadcasted_iota(jnp.int32, (8, 128), 1)
    odd = (lane & 32) != 0
    high = lane >= 64
    skewed = [skew(x, odd, high) for x in groups]
    turned = [[w[0]] + [pltpu.roll(w[d], 32 * d, 1) for d in range(1, 4)] for w in skewed]
    back = [skew(w, odd, high) for w in turned]
    return [(w[0], w[3], w[2], w[1]) for w in back]


BLOCKS = [(f, qx, g) for f in range(6) for qx in range(2) for g in range(2)]
INNER = 7
INNER_ROWS = 6 * INNER


def edges_kernel(state, land, low_out, high_out, top, bottom, land_top, land_bottom, sems):
    copies = [
        pltpu.make_async_copy(state.at[:, :, 0:8, :], top, sems.at[0]),
        pltpu.make_async_copy(state.at[:, :, 56:64, :], bottom, sems.at[1]),
        pltpu.make_async_copy(land.at[0:8, :], land_top, sems.at[2]),
        pltpu.make_async_copy(land.at[56:64, :], land_bottom, sems.at[3]),
    ]
    for copy in copies:
        copy.start()
    for copy in copies:
        copy.wait()
    low_out[24] = land_bottom[8 - HALO :, :].astype(jnp.float32)
    high_out[24] = land_top[:HALO, :].astype(jnp.float32)
    for m in range(4):
        for f in range(6):
            low_out[6 * m + f] = bottom[m, f, 8 - HALO :, :]
            high_out[6 * m + f] = top[m, f, :HALO, :]


CUTS = (0, 40, 80, 120, 168)


def inner_kernel(state, land, out, begin, land_ref, packed, fields_ref, sems):
    arrive = [pltpu.make_async_copy(land, land_ref, sems.at[0])]
    arrive += [pltpu.make_async_copy(state.at[m], begin.at[m], sems.at[1 + m]) for m in range(4)]
    leave = [
        pltpu.make_async_copy(
            packed.at[:, pl.ds(CUTS[m], CUTS[m + 1] - CUTS[m]), :],
            out.at[:, pl.ds(CUTS[m], CUTS[m + 1] - CUTS[m]), :],
            sems.at[5 + m],
        )
        for m in range(4)
    ]
    for copy in arrive:
        copy.start()
    arrive[0].wait()
    mask = land_ref[...].astype(jnp.float32)
    mask = jnp.concatenate([mask, mask], axis=0)
    for pair in range(2):
        members = (2 * pair, 2 * pair + 1)
        for m in members:
            arrive[1 + m].wait()
        fields = forecast(
            tuple(jnp.concatenate([begin[m, f] for m in members], axis=0) for f in range(6)), mask
        )
        for m in members:
            for f in range(6):
                for g in range(2):
                    fields_ref[m % 2, f, g] = fields[f][g][64 * (m % 2) : 64 * (m % 2) + 64]
        for m in members:
            for i in range(0, len(BLOCKS), 12):
                todo = BLOCKS[i : i + 12]
                tiles = swap_blocks(
                    [
                        [
                            fields_ref[m % 2, f, g, pl.ds((4, 32)[qx] + a, 8, stride=4), :]
                            for a in range(4)
                        ]
                        for f, qx, g in todo
                    ]
                )
                for (f, qx, g), z in zip(todo, tiles):
                    row = m * INNER_ROWS + f * INNER
                    for b in range(4):
                        packed[qx * 8 + g * 4 + b, row : row + INNER, :] = z[b][0:INNER]
            leave[m].start()
    for copy in leave:
        copy.wait()


def outer_kernel(state, land, from_low, from_high, packed, ocean, fields_ref):
    mask = jnp.concatenate(
        [
            land[0:16, :].astype(jnp.float32),
            land[48:64, :].astype(jnp.float32),
            from_high[24],
            from_low[24],
        ],
        axis=0,
    )

    def one(m, carry):
        begin = tuple(
            jnp.concatenate(
                [state[m, f, 0:16, :], state[m, f, 48:64, :], from_high[6 * m + f], from_low[6 * m + f]],
                axis=0,
            )
            for f in range(6)
        )
        fields = forecast(begin, mask)
        for f in range(6):
            for g in range(2):
                sides = jnp.concatenate([fields[f][g][0:4], fields[f][g][28:32]], axis=0)
                fields_ref[g, pl.ds(pl.multiple_of((6 * m + f) * 8, 8), 8), :] = sides
        return carry

    lax.fori_loop(0, 4, one, 0)
    for g in range(2):
        ocean[g] = land[:, 128 * g : 128 * g + 128].astype(jnp.float32)
    todo = [(i, qx, g) for i in range(3) for qx in range(2) for g in range(2)]
    tiles = swap_blocks(
        [
            [fields_ref[g, pl.ds(64 * i + 4 * qx + a, 8, stride=8), :] for a in range(4)]
            for i, qx, g in todo
        ]
    )
    for (i, qx, g), z in zip(todo, tiles):
        for b in range(4):
            packed[qx * 8 + g * 4 + b, 8 * i : 8 * i + 8, :] = z[b]


def places(index, members):
    chosen = index[...]
    side = lax.axis_index("member") // 8
    field = chosen >> 10
    group = ((chosen >> 7) + side) & 7
    row = jnp.where(group == 0, INNER_ROWS + field, field * INNER + group - 1)
    lane = chosen & 127
    halves = [slice(0, 128), slice(128, 256)]
    return (
        [jnp.broadcast_to(row[:, half], (members, 128)) for half in halves],
        [jnp.broadcast_to(lane[:, half], (members, 128)) for half in halves],
    )


def pick(tile, r, rows_of, lanes_of, acc):
    return tuple(
        jnp.where(rows_of[half] == r, jnp.take_along_axis(tile, lanes_of[half], axis=1), acc[half])
        for half in range(2)
    )


def split(x):
    members = x.shape[0]
    dev = x - jnp.sum(x, axis=0, keepdims=True) * (1.0 / members)
    high = dev.astype(jnp.bfloat16)
    return high, (dev - high.astype(jnp.float32)).astype(jnp.bfloat16)


def gather_kernel(x_ref, index, observed, dev_ref):
    members = 64
    rows_of, lanes_of = places(index, members)

    def scan(block, acc):
        rows = [block * SCAN + i for i in range(SCAN)]
        tiles = [x_ref[pl.ds(r, members, stride=INNER_ROWS), :] for r in rows]
        for r, tile in zip(rows, tiles):
            acc = pick(tile, r, rows_of, lanes_of, acc)
        for r, tile in zip(rows, tiles):
            high, low = split(tile)
            dev_ref[r, 0:members, :] = high
            dev_ref[r, members:, :] = low
        return acc

    zero = jnp.zeros((members, 128), jnp.float32)
    acc = lax.fori_loop(0, INNER_ROWS // SCAN, scan, (zero, zero))
    observed[:, 0:128] = acc[0]
    observed[:, 128:256] = acc[1]


def analysis_kernel(
    x_ref, picked, dev_ref, index, count, values, errors, out_ref, outer_ref
):
    members = 64
    rows_of, lanes_of = places(index, members)
    acc = (picked[:, 0:128], picked[:, 128:256])
    for f in range(6):
        tile = x_ref[pl.ds(f, members, stride=6), :]
        acc = pick(tile, INNER_ROWS + f, rows_of, lanes_of, acc)
        high, low = split(tile)
        outer_ref[f, 0:members, :] = high
        outer_ref[f, members:, :] = low
    observed = jnp.concatenate(acc, axis=1)
    obs_mean = jnp.sum(observed, axis=0, keepdims=True) * (1.0 / members)
    spread = observed - obs_mean
    slots = lax.broadcasted_iota(jnp.int32, (1, 256), 1)
    weight = jnp.where(slots < count[...], 1.0 / errors[...], 0.0)
    innovation = values[...] - obs_mean
    scaled = spread * weight
    column = lax.broadcasted_iota(jnp.int32, (members, 2 * members), 1)
    line = lax.broadcasted_iota(jnp.int32, (members, 2 * members), 0)
    twice = (line == (column & (members - 1))).astype(jnp.float32)
    once = (line == column).astype(jnp.float32)

    def parts(a, count=3):
        found = []
        for _ in range(count):
            found.append(a.astype(jnp.bfloat16))
            a = a - found[-1].astype(jnp.float32)
        return found

    nothing = jnp.zeros((members, 2 * members), jnp.bfloat16)

    def times(a, b):
        (ah, am, al), (bh, bm, bl) = a, b
        coarse = jnp.dot(
            jnp.concatenate([ah, am], axis=1),
            jnp.concatenate([bh, bm, bh, bm], axis=0),
            preferred_element_type=jnp.float32,
        )
        fine = jnp.dot(
            jnp.concatenate([al, ah], axis=1),
            jnp.concatenate([bh, bm, bl, nothing], axis=0),
            preferred_element_type=jnp.float32,
        )
        return coarse + fine

    def over_slots(a, b):
        return lax.dot_general(
            a,
            jnp.concatenate([b, b], axis=0),
            (((1,), (1,)), ((), ())),
            preferred_element_type=jnp.float32,
        )

    (ah, am, al), (bh, bm, bl) = parts(scaled), parts(spread)
    gram = over_slots(ah, bh) + (
        (over_slots(ah, bm) + over_slots(am, bh))
        + (over_slots(am, bm) + over_slots(ah, bl) + over_slots(al, bh))
    )
    moved = jnp.sum(once * jnp.sum(scaled * innovation, axis=1, keepdims=True), axis=0, keepdims=True)
    system = (members - 1.0) * twice + gram
    system_parts = parts(system)
    square = times(system_parts, system_parts)
    total = 0.5 * jnp.sum(jnp.sum(system * system, axis=0, keepdims=True), axis=1, keepdims=True)
    norm_inv = lax.rsqrt(total)
    norm_inv_root = jnp.sqrt(norm_inv)
    root = system * norm_inv
    inverse = 1.5 * twice - 0.5 * root
    root = 1.5 * root - 0.5 * (square * norm_inv * norm_inv)
    for sweep in range(1, NS_ITERS):
        root_parts, inverse_parts = parts(root), parts(inverse)
        factor = 1.5 * twice - 0.5 * times(inverse_parts, root_parts)
        factor_parts = parts(factor)
        if sweep < NS_ITERS - 1:
            root = times(root_parts, factor_parts)
            inverse = times(factor_parts, inverse_parts)
    left_half = (column[0:1] < members).astype(jnp.float32)
    weights = moved
    for _ in range(2):
        step_one = jnp.sum(inverse * weights, axis=1, keepdims=True)
        weights = jnp.sum(factor * step_one, axis=0, keepdims=True) * left_half
    weights = weights + pltpu.roll(weights, members, 1)
    sqrt_inv = times(factor_parts, inverse_parts) * norm_inv_root
    flipped = weights * norm_inv + math.sqrt(members - 1.0) * sqrt_inv - twice
    left = jnp.concatenate(parts(flipped, 2), axis=1)

    def apply(pair_of, places_of):
        results = []
        for pair in pair_of:
            right = jnp.concatenate([pair, pair], axis=0)
            results.append(jnp.dot(left, right, preferred_element_type=jnp.float32))
        for result, rows in zip(results, places_of):
            for j in range(2):
                out_ref[pl.ds(rows[j], members, stride=48), :] = result[:, 128 * j : 128 * j + 128]

    for i in range(3):
        first = 2 * INNER * i
        pairs = [
            jnp.concatenate([dev_ref[first + 2 * k], dev_ref[first + 2 * k + 1]], axis=1)
            for k in range(INNER)
        ]
        pairs.append(jnp.concatenate([outer_ref[2 * i], outer_ref[2 * i + 1]], axis=1))
        spots = [[r + r // INNER + 1 for r in (first + 2 * k, first + 2 * k + 1)] for k in range(INNER)]
        spots.append([16 * i, 16 * i + 8])
        apply(pairs, spots)


def unpack_kernel(packed, land, out, field, sems):
    copies = [
        pltpu.make_async_copy(field.at[m, :, g], out.at[m, :, :, pl.ds(128 * g, 128)], sems.at[m, g])
        for m in range(4)
        for g in range(2)
    ]
    masks = {}
    for qx in range(2):
        for g in range(2):
            for a in range(4):
                rows = land[g, pl.ds(32 * qx + a, 8, stride=4), :]
                masks[qx, g, a] = rows
    for m in range(4):
        for i in range(0, len(BLOCKS), 12):
            todo = BLOCKS[i : i + 12]
            tiles = swap_blocks(
                [
                    [
                        packed[qx * 8 + g * 4 + b, 48 * m + 8 * f : 48 * m + 8 * f + 8, :]
                        for b in range(4)
                    ]
                    for f, qx, g in todo
                ]
            )
            for (f, qx, g), z in zip(todo, tiles):
                for a in range(4):
                    tile = pltpu.roll(z[a], 7, 0) if qx else z[a]
                    field[m, f, g, pl.ds(32 * qx + a, 8, stride=4), :] = tile * masks[qx, g, a]
        for g in range(2):
            copies[2 * m + g].start()
    for copy in copies:
        copy.wait()


def shape(*dims):
    return jax.ShapeDtypeStruct(dims, jnp.float32)


def local(initial_realizations, land_mask, obs_index, obs_count, obs_value, obs_error):
    whole = pl.BlockSpec(memory_space=pltpu.VMEM)
    far = pl.BlockSpec(memory_space=pltpu.HBM)
    to_high, to_low = pl.pallas_call(
        edges_kernel,
        out_shape=[shape(25, HALO, 256)] * 2,
        in_specs=[far, far],
        out_specs=[whole, whole],
        scratch_shapes=[
            pltpu.VMEM((4, 6, 8, 256), jnp.float32),
            pltpu.VMEM((4, 6, 8, 256), jnp.float32),
            pltpu.VMEM((8, 256), jnp.int32),
            pltpu.VMEM((8, 256), jnp.int32),
            pltpu.SemaphoreType.DMA((4,)),
        ],
        cost_estimate=pl.CostEstimate(flops=100000, bytes_accessed=800000, transcendentals=0),
    )(initial_realizations, land_mask)
    count = lax.axis_size("domain")
    forward = [(i, (i + 1) % count) for i in range(count)]
    backward = [(target, source) for source, target in forward]
    from_low = lax.ppermute(to_high, "domain", forward)
    from_high = lax.ppermute(to_low, "domain", backward)
    inner = pl.pallas_call(
        inner_kernel,
        out_shape=shape(16, 4 * INNER_ROWS, 128),
        in_specs=[far, far],
        out_specs=far,
        scratch_shapes=[
            pltpu.VMEM((4, 6, 64, 256), jnp.float32),
            pltpu.VMEM((64, 256), jnp.int32),
            pltpu.VMEM((16, 4 * INNER_ROWS, 128), jnp.float32),
            pltpu.VMEM((2, 6, 2, 64, 128), jnp.float32),
            pltpu.SemaphoreType.DMA((9,)),
        ],
        compiler_params=pltpu.CompilerParams(vmem_limit_bytes=WHOLE_VMEM),
        cost_estimate=pl.CostEstimate(flops=20000000, bytes_accessed=3000000, transcendentals=0),
    )(initial_realizations, land_mask)
    outer, ocean = pl.pallas_call(
        outer_kernel,
        out_shape=[shape(16, 24, 128), shape(2, 64, 128)],
        in_specs=[whole] * 4,
        out_specs=[whole] * 2,
        scratch_shapes=[pltpu.VMEM((2, 192, 128), jnp.float32)],
        compiler_params=pltpu.CompilerParams(vmem_limit_bytes=VMEM_LIMIT),
        cost_estimate=pl.CostEstimate(flops=10000000, bytes_accessed=3000000, transcendentals=0),
    )(initial_realizations, land_mask, from_low, from_high)
    inner = lax.all_to_all(inner, "member", split_axis=0, concat_axis=0, tiled=True)
    outer = lax.all_to_all(outer, "member", split_axis=0, concat_axis=0, tiled=True)
    observed, deviations = pl.pallas_call(
        gather_kernel,
        out_shape=[shape(64, 256), jax.ShapeDtypeStruct((INNER_ROWS, 128, 128), jnp.bfloat16)],
        in_specs=[whole] * 2,
        out_specs=[whole] * 2,
        compiler_params=pltpu.CompilerParams(vmem_limit_bytes=VMEM_LIMIT),
        cost_estimate=pl.CostEstimate(flops=10000000, bytes_accessed=3000000, transcendentals=0),
    )(inner.reshape(64 * INNER_ROWS, 128), obs_index[0])
    increment = pl.pallas_call(
        analysis_kernel,
        out_shape=shape(3072, 128),
        in_specs=[whole] * 7,
        out_specs=whole,
        scratch_shapes=[pltpu.VMEM((6, 128, 128), jnp.bfloat16)],
        compiler_params=pltpu.CompilerParams(vmem_limit_bytes=VMEM_LIMIT),
        cost_estimate=pl.CostEstimate(flops=60000000, bytes_accessed=3000000, transcendentals=0),
    )(
        outer.reshape(384, 128),
        observed,
        deviations,
        obs_index[0],
        obs_count,
        obs_value[0],
        obs_error[0],
    )
    returned = lax.all_to_all(
        increment.reshape(16, 192, 128), "member", split_axis=0, concat_axis=0, tiled=True
    )
    return pl.pallas_call(
        unpack_kernel,
        out_shape=shape(4, 6, 64, 256),
        in_specs=[whole, whole],
        out_specs=far,
        scratch_shapes=[pltpu.VMEM((4, 6, 2, 64, 128), jnp.float32), pltpu.SemaphoreType.DMA((4, 2))],
        compiler_params=pltpu.CompilerParams(vmem_limit_bytes=VMEM_LIMIT),
    )(returned, ocean)


def solution(mesh):
    in_specs = (
        P("member", None, "domain", None),
        P("domain", None),
        P("domain", "member", None),
        P("domain", "member"),
        P("domain", "member", None),
        P("domain", "member", None),
    )
    out_specs = P("member", None, "domain", None)
    return jax.shard_map(local, mesh=mesh, in_specs=in_specs, out_specs=out_specs, check_vma=False)
```

```python
import math

import jax
import jax.numpy as jnp
from jax import lax
from jax.experimental import pallas as pl
from jax.experimental.pallas import tpu as pltpu
from jax.sharding import PartitionSpec as P

NS_ITERS = 8
CORIOLIS = 0.1
STRATIFY = 1.5
HALO = 4
SCAN = 14
VMEM_LIMIT = 48 * 1024 * 1024
WHOLE_VMEM = 62 * 1024 * 1024


def east(field):
    return tuple(pltpu.roll(x, x.shape[0] - 1, 0) - pltpu.roll(x, 1, 0) for x in field)


def north(field, first, last):
    west, rest = field
    west_up, rest_up = pltpu.roll(west, 1, 1), pltpu.roll(rest, 1, 1)
    west_down, rest_down = pltpu.roll(west, 127, 1), pltpu.roll(rest, 127, 1)
    return (
        jnp.where(last, rest_down, west_down) - jnp.where(first, 0.0, west_up),
        jnp.where(last, 0.0, rest_down) - jnp.where(first, west_up, rest_up),
    )


def step(state, mask, first, last):
    u1, v1, h1, u2, v2, h2 = state
    halves = range(2)
    du, dv = east(u1), north(v1, first, last)
    h1 = tuple(h1[i] - 0.125 * (du[i] + dv[i]) for i in halves)
    du, dv = east(u2), north(v2, first, last)
    h2 = tuple(h2[i] - 0.0625 * (du[i] + dv[i]) for i in halves)

    def turn(u, v, p):
        px, py = east(p), north(p, first, last)
        return (
            tuple((u[i] + CORIOLIS * v[i] - 0.125 * px[i]) * mask[i] for i in halves),
            tuple((v[i] - CORIOLIS * u[i] - 0.125 * py[i]) * mask[i] for i in halves),
        )

    u1, v1 = turn(u1, v1, tuple(h1[i] + h2[i] for i in halves))
    u2, v2 = turn(u2, v2, tuple(h1[i] + STRATIFY * h2[i] for i in halves))
    return (u1, v1, h1, u2, v2, h2)


def halves_of(x):
    return (x[..., 0:128], x[..., 128:256])


def forecast(state, mask):
    lane = lax.broadcasted_iota(jnp.int32, mask.shape[:1] + (128,), 1)
    first = lane == 0
    last = lane == 127
    state = tuple(halves_of(x) for x in state)
    mask = halves_of(mask)
    for _ in range(2):
        state = step(state, mask, first, last)
    return state


def skew(x, odd, high):
    once = [jnp.where(odd, x[(i + 1) % 4], x[i]) for i in range(4)]
    return [jnp.where(high, once[(i + 2) % 4], once[i]) for i in range(4)]


def swap_blocks(groups):
    lane = lax.broadcasted_iota(jnp.int32, (8, 128), 1)
    odd = (lane & 32) != 0
    high = lane >= 64
    skewed = [skew(x, odd, high) for x in groups]
    turned = [[w[0]] + [pltpu.roll(w[d], 32 * d, 1) for d in range(1, 4)] for w in skewed]
    back = [skew(w, odd, high) for w in turned]
    return [(w[0], w[3], w[2], w[1]) for w in back]


BLOCKS = [(f, qx, g) for f in range(6) for qx in range(2) for g in range(2)]
INNER = 7
INNER_ROWS = 6 * INNER


def edges_kernel(state, land, low_out, high_out, top, bottom, land_top, land_bottom, sems):
    copies = [
        pltpu.make_async_copy(state.at[:, :, 0:8, :], top, sems.at[0]),
        pltpu.make_async_copy(state.at[:, :, 56:64, :], bottom, sems.at[1]),
        pltpu.make_async_copy(land.at[0:8, :], land_top, sems.at[2]),
        pltpu.make_async_copy(land.at[56:64, :], land_bottom, sems.at[3]),
    ]
    for copy in copies:
        copy.start()
    for copy in copies:
        copy.wait()
    low_out[24] = land_bottom[8 - HALO :, :].astype(jnp.float32)
    high_out[24] = land_top[:HALO, :].astype(jnp.float32)
    for m in range(4):
        for f in range(6):
            low_out[6 * m + f] = bottom[m, f, 8 - HALO :, :]
            high_out[6 * m + f] = top[m, f, :HALO, :]


CUTS = (0, 40, 80, 120, 168)


def inner_kernel(state, land, out, begin, land_ref, packed, fields_ref, sems):
    arrive = [pltpu.make_async_copy(land, land_ref, sems.at[0])]
    arrive += [pltpu.make_async_copy(state.at[m], begin.at[m], sems.at[1 + m]) for m in range(4)]
    leave = [
        pltpu.make_async_copy(
            packed.at[:, pl.ds(CUTS[m], CUTS[m + 1] - CUTS[m]), :],
            out.at[:, pl.ds(CUTS[m], CUTS[m + 1] - CUTS[m]), :],
            sems.at[5 + m],
        )
        for m in range(4)
    ]
    for copy in arrive:
        copy.start()
    arrive[0].wait()
    mask = land_ref[...].astype(jnp.float32)
    mask = jnp.concatenate([mask, mask], axis=0)
    for pair in range(2):
        members = (2 * pair, 2 * pair + 1)
        for m in members:
            arrive[1 + m].wait()
        fields = forecast(
            tuple(jnp.concatenate([begin[m, f] for m in members], axis=0) for f in range(6)), mask
        )
        for m in members:
            for f in range(6):
                for g in range(2):
                    fields_ref[m % 2, f, g] = fields[f][g][64 * (m % 2) : 64 * (m % 2) + 64]
        for m in members:
            for i in range(0, len(BLOCKS), 12):
                todo = BLOCKS[i : i + 12]
                tiles = swap_blocks(
                    [
                        [
                            fields_ref[m % 2, f, g, pl.ds((4, 32)[qx] + a, 8, stride=4), :]
                            for a in range(4)
                        ]
                        for f, qx, g in todo
                    ]
                )
                for (f, qx, g), z in zip(todo, tiles):
                    row = m * INNER_ROWS + f * INNER
                    for b in range(4):
                        packed[qx * 8 + g * 4 + b, row : row + INNER, :] = z[b][0:INNER]
            leave[m].start()
    for copy in leave:
        copy.wait()


def outer_kernel(state, land, from_low, from_high, packed, ocean, fields_ref):
    mask = jnp.concatenate(
        [
            land[0:16, :].astype(jnp.float32),
            land[48:64, :].astype(jnp.float32),
            from_high[24],
            from_low[24],
        ],
        axis=0,
    )

    def one(m, carry):
        begin = tuple(
            jnp.concatenate(
                [state[m, f, 0:16, :], state[m, f, 48:64, :], from_high[6 * m + f], from_low[6 * m + f]],
                axis=0,
            )
            for f in range(6)
        )
        fields = forecast(begin, mask)
        for f in range(6):
            for g in range(2):
                sides = jnp.concatenate([fields[f][g][0:4], fields[f][g][28:32]], axis=0)
                fields_ref[g, pl.ds(pl.multiple_of((6 * m + f) * 8, 8), 8), :] = sides
        return carry

    lax.fori_loop(0, 4, one, 0)
    for g in range(2):
        ocean[g] = land[:, 128 * g : 128 * g + 128].astype(jnp.float32)
    todo = [(i, qx, g) for i in range(3) for qx in range(2) for g in range(2)]
    tiles = swap_blocks(
        [
            [fields_ref[g, pl.ds(64 * i + 4 * qx + a, 8, stride=8), :] for a in range(4)]
            for i, qx, g in todo
        ]
    )
    for (i, qx, g), z in zip(todo, tiles):
        for b in range(4):
            packed[qx * 8 + g * 4 + b, 8 * i : 8 * i + 8, :] = z[b]


def places(index, members):
    chosen = index[...]
    side = lax.axis_index("member") // 8
    field = chosen >> 10
    group = ((chosen >> 7) + side) & 7
    row = jnp.where(group == 0, INNER_ROWS + field, field * INNER + group - 1)
    lane = chosen & 127
    halves = [slice(0, 128), slice(128, 256)]
    return (
        [jnp.broadcast_to(row[:, half], (members, 128)) for half in halves],
        [jnp.broadcast_to(lane[:, half], (members, 128)) for half in halves],
    )


def pick(tile, r, rows_of, lanes_of, acc):
    return tuple(
        jnp.where(rows_of[half] == r, jnp.take_along_axis(tile, lanes_of[half], axis=1), acc[half])
        for half in range(2)
    )


def split(x):
    members = x.shape[0]
    dev = x - jnp.sum(x, axis=0, keepdims=True) * (1.0 / members)
    high = dev.astype(jnp.bfloat16)
    return high, (dev - high.astype(jnp.float32)).astype(jnp.bfloat16)


def gather_kernel(x_ref, index, observed, dev_ref):
    members = 64
    rows_of, lanes_of = places(index, members)

    def scan(block, acc):
        rows = [block * SCAN + i for i in range(SCAN)]
        tiles = [x_ref[pl.ds(r, members, stride=INNER_ROWS), :] for r in rows]
        for r, tile in zip(rows, tiles):
            acc = pick(tile, r, rows_of, lanes_of, acc)
        for r, tile in zip(rows, tiles):
            high, low = split(tile)
            dev_ref[r, 0:members, :] = high
            dev_ref[r, members:, :] = low
        return acc

    zero = jnp.zeros((members, 128), jnp.float32)
    acc = lax.fori_loop(0, INNER_ROWS // SCAN, scan, (zero, zero))
    observed[:, 0:128] = acc[0]
    observed[:, 128:256] = acc[1]


def analysis_kernel(
    x_ref, picked, dev_ref, index, count, values, errors, out_ref, outer_ref
):
    members = 64
    rows_of, lanes_of = places(index, members)
    acc = (picked[:, 0:128], picked[:, 128:256])
    for f in range(6):
        tile = x_ref[pl.ds(f, members, stride=6), :]
        acc = pick(tile, INNER_ROWS + f, rows_of, lanes_of, acc)
        high, low = split(tile)
        outer_ref[f, 0:members, :] = high
        outer_ref[f, members:, :] = low
    observed = jnp.concatenate(acc, axis=1)
    obs_mean = jnp.sum(observed, axis=0, keepdims=True) * (1.0 / members)
    spread = observed - obs_mean
    slots = lax.broadcasted_iota(jnp.int32, (1, 256), 1)
    weight = jnp.where(slots < count[...], 1.0 / errors[...], 0.0)
    innovation = values[...] - obs_mean
    scaled = spread * weight
    column = lax.broadcasted_iota(jnp.int32, (members, 2 * members), 1)
    line = lax.broadcasted_iota(jnp.int32, (members, 2 * members), 0)
    twice = (line == (column & (members - 1))).astype(jnp.float32)
    once = (line == column).astype(jnp.float32)

    def parts(a, count=3):
        found = []
        for _ in range(count):
            found.append(a.astype(jnp.bfloat16))
            a = a - found[-1].astype(jnp.float32)
        return found

    nothing = jnp.zeros((members, 2 * members), jnp.bfloat16)

    def times(a, b):
        (ah, am, al), (bh, bm, bl) = a, b
        coarse = jnp.dot(
            jnp.concatenate([ah, am], axis=1),
            jnp.concatenate([bh, bm, bh, bm], axis=0),
            preferred_element_type=jnp.float32,
        )
        fine = jnp.dot(
            jnp.concatenate([al, ah], axis=1),
            jnp.concatenate([bh, bm, bl, nothing], axis=0),
            preferred_element_type=jnp.float32,
        )
        return coarse + fine

    def over_slots(a, b):
        return lax.dot_general(
            a,
            jnp.concatenate([b, b], axis=0),
            (((1,), (1,)), ((), ())),
            preferred_element_type=jnp.float32,
        )

    (ah, am, al), (bh, bm, bl) = parts(scaled), parts(spread)
    gram = over_slots(ah, bh) + (
        (over_slots(ah, bm) + over_slots(am, bh))
        + (over_slots(am, bm) + over_slots(ah, bl) + over_slots(al, bh))
    )
    moved = jnp.sum(once * jnp.sum(scaled * innovation, axis=1, keepdims=True), axis=0, keepdims=True)
    system = (members - 1.0) * twice + gram
    system_parts = parts(system)
    square = times(system_parts, system_parts)
    total = 0.5 * jnp.sum(jnp.sum(system * system, axis=0, keepdims=True), axis=1, keepdims=True)
    norm_inv = lax.rsqrt(total)
    norm_inv_root = jnp.sqrt(norm_inv)
    root = system * norm_inv
    inverse = 1.5 * twice - 0.5 * root
    root = 1.5 * root - 0.5 * (square * norm_inv * norm_inv)
    for sweep in range(1, NS_ITERS):
        root_parts, inverse_parts = parts(root), parts(inverse)
        factor = 1.5 * twice - 0.5 * times(inverse_parts, root_parts)
        factor_parts = parts(factor)
        if sweep < NS_ITERS - 1:
            root = times(root_parts, factor_parts)
            inverse = times(factor_parts, inverse_parts)
    left_half = (column[0:1] < members).astype(jnp.float32)
    weights = moved
    for _ in range(2):
        step_one = jnp.sum(inverse * weights, axis=1, keepdims=True)
        weights = jnp.sum(factor * step_one, axis=0, keepdims=True) * left_half
    weights = weights + pltpu.roll(weights, members, 1)
    sqrt_inv = times(factor_parts, inverse_parts) * norm_inv_root
    flipped = weights * norm_inv + math.sqrt(members - 1.0) * sqrt_inv - twice
    left = jnp.concatenate(parts(flipped, 2), axis=0)

    def apply(pair_of, places_of):
        results = []
        for pair in pair_of:
            both = jnp.dot(left, pair, preferred_element_type=jnp.float32)
            results.append(both[0:members] + both[members:])
        for result, rows in zip(results, places_of):
            for j in range(2):
                out_ref[pl.ds(rows[j], members, stride=48), :] = result[:, 128 * j : 128 * j + 128]

    for i in range(3):
        first = 2 * INNER * i
        pairs = [
            jnp.concatenate([dev_ref[first + 2 * k], dev_ref[first + 2 * k + 1]], axis=1)
            for k in range(INNER)
        ]
        pairs.append(jnp.concatenate([outer_ref[2 * i], outer_ref[2 * i + 1]], axis=1))
        spots = [[r + r // INNER + 1 for r in (first + 2 * k, first + 2 * k + 1)] for k in range(INNER)]
        spots.append([16 * i, 16 * i + 8])
        apply(pairs, spots)


def unpack_kernel(packed, land, out, field, sems):
    copies = [
        pltpu.make_async_copy(field.at[m, :, g], out.at[m, :, :, pl.ds(128 * g, 128)], sems.at[m, g])
        for m in range(4)
        for g in range(2)
    ]
    masks = {}
    for qx in range(2):
        for g in range(2):
            for a in range(4):
                rows = land[g, pl.ds(32 * qx + a, 8, stride=4), :]
                masks[qx, g, a] = rows
    for m in range(4):
        for i in range(0, len(BLOCKS), 12):
            todo = BLOCKS[i : i + 12]
            tiles = swap_blocks(
                [
                    [
                        packed[qx * 8 + g * 4 + b, 48 * m + 8 * f : 48 * m + 8 * f + 8, :]
                        for b in range(4)
                    ]
                    for f, qx, g in todo
                ]
            )
            for (f, qx, g), z in zip(todo, tiles):
                for a in range(4):
                    tile = pltpu.roll(z[a], 7, 0) if qx else z[a]
                    field[m, f, g, pl.ds(32 * qx + a, 8, stride=4), :] = tile * masks[qx, g, a]
        for g in range(2):
            copies[2 * m + g].start()
    for copy in copies:
        copy.wait()


def shape(*dims):
    return jax.ShapeDtypeStruct(dims, jnp.float32)


def local(initial_realizations, land_mask, obs_index, obs_count, obs_value, obs_error):
    whole = pl.BlockSpec(memory_space=pltpu.VMEM)
    far = pl.BlockSpec(memory_space=pltpu.HBM)
    to_high, to_low = pl.pallas_call(
        edges_kernel,
        out_shape=[shape(25, HALO, 256)] * 2,
        in_specs=[far, far],
        out_specs=[whole, whole],
        scratch_shapes=[
            pltpu.VMEM((4, 6, 8, 256), jnp.float32),
            pltpu.VMEM((4, 6, 8, 256), jnp.float32),
            pltpu.VMEM((8, 256), jnp.int32),
            pltpu.VMEM((8, 256), jnp.int32),
            pltpu.SemaphoreType.DMA((4,)),
        ],
        cost_estimate=pl.CostEstimate(flops=100000, bytes_accessed=800000, transcendentals=0),
    )(initial_realizations, land_mask)
    count = lax.axis_size("domain")
    forward = [(i, (i + 1) % count) for i in range(count)]
    backward = [(target, source) for source, target in forward]
    from_low = lax.ppermute(to_high, "domain", forward)
    from_high = lax.ppermute(to_low, "domain", backward)
    inner = pl.pallas_call(
        inner_kernel,
        out_shape=shape(16, 4 * INNER_ROWS, 128),
        in_specs=[far, far],
        out_specs=far,
        scratch_shapes=[
            pltpu.VMEM((4, 6, 64, 256), jnp.float32),
            pltpu.VMEM((64, 256), jnp.int32),
            pltpu.VMEM((16, 4 * INNER_ROWS, 128), jnp.float32),
            pltpu.VMEM((2, 6, 2, 64, 128), jnp.float32),
            pltpu.SemaphoreType.DMA((9,)),
        ],
        compiler_params=pltpu.CompilerParams(vmem_limit_bytes=WHOLE_VMEM),
        cost_estimate=pl.CostEstimate(flops=20000000, bytes_accessed=3000000, transcendentals=0),
    )(initial_realizations, land_mask)
    outer, ocean = pl.pallas_call(
        outer_kernel,
        out_shape=[shape(16, 24, 128), shape(2, 64, 128)],
        in_specs=[whole] * 4,
        out_specs=[whole] * 2,
        scratch_shapes=[pltpu.VMEM((2, 192, 128), jnp.float32)],
        compiler_params=pltpu.CompilerParams(vmem_limit_bytes=VMEM_LIMIT),
        cost_estimate=pl.CostEstimate(flops=10000000, bytes_accessed=3000000, transcendentals=0),
    )(initial_realizations, land_mask, from_low, from_high)
    inner = lax.all_to_all(inner, "member", split_axis=0, concat_axis=0, tiled=True)
    outer = lax.all_to_all(outer, "member", split_axis=0, concat_axis=0, tiled=True)
    observed, deviations = pl.pallas_call(
        gather_kernel,
        out_shape=[shape(64, 256), jax.ShapeDtypeStruct((INNER_ROWS, 128, 128), jnp.bfloat16)],
        in_specs=[whole] * 2,
        out_specs=[whole] * 2,
        compiler_params=pltpu.CompilerParams(vmem_limit_bytes=VMEM_LIMIT),
        cost_estimate=pl.CostEstimate(flops=10000000, bytes_accessed=3000000, transcendentals=0),
    )(inner.reshape(64 * INNER_ROWS, 128), obs_index[0])
    increment = pl.pallas_call(
        analysis_kernel,
        out_shape=shape(3072, 128),
        in_specs=[whole] * 7,
        out_specs=whole,
        scratch_shapes=[pltpu.VMEM((6, 128, 128), jnp.bfloat16)],
        compiler_params=pltpu.CompilerParams(vmem_limit_bytes=VMEM_LIMIT),
        cost_estimate=pl.CostEstimate(flops=60000000, bytes_accessed=3000000, transcendentals=0),
    )(
        outer.reshape(384, 128),
        observed,
        deviations,
        obs_index[0],
        obs_count,
        obs_value[0],
        obs_error[0],
    )
    returned = lax.all_to_all(
        increment.reshape(16, 192, 128), "member", split_axis=0, concat_axis=0, tiled=True
    )
    return pl.pallas_call(
        unpack_kernel,
        out_shape=shape(4, 6, 64, 256),
        in_specs=[whole, whole],
        out_specs=far,
        scratch_shapes=[pltpu.VMEM((4, 6, 2, 64, 128), jnp.float32), pltpu.SemaphoreType.DMA((4, 2))],
        compiler_params=pltpu.CompilerParams(vmem_limit_bytes=VMEM_LIMIT),
    )(returned, ocean)


def solution(mesh):
    in_specs = (
        P("member", None, "domain", None),
        P("domain", None),
        P("domain", "member", None),
        P("domain", "member"),
        P("domain", "member", None),
        P("domain", "member", None),
    )
    out_specs = P("member", None, "domain", None)
    return jax.shard_map(local, mesh=mesh, in_specs=in_specs, out_specs=out_specs, check_vma=False)
```

```python
import math

import jax
import jax.numpy as jnp
from jax import lax
from jax.experimental import pallas as pl
from jax.experimental.pallas import tpu as pltpu
from jax.sharding import PartitionSpec as P

NS_ITERS = 8
CORIOLIS = 0.1
STRATIFY = 1.5
HALO = 4
SCAN = 14
VMEM_LIMIT = 48 * 1024 * 1024
WHOLE_VMEM = 62 * 1024 * 1024


def east(field):
    return tuple(pltpu.roll(x, x.shape[0] - 1, 0) - pltpu.roll(x, 1, 0) for x in field)


def north(field, first, last):
    west, rest = field
    west_up, rest_up = pltpu.roll(west, 1, 1), pltpu.roll(rest, 1, 1)
    west_down, rest_down = pltpu.roll(west, 127, 1), pltpu.roll(rest, 127, 1)
    return (
        jnp.where(last, rest_down, west_down) - jnp.where(first, 0.0, west_up),
        jnp.where(last, 0.0, rest_down) - jnp.where(first, west_up, rest_up),
    )


def step(state, mask, first, last):
    u1, v1, h1, u2, v2, h2 = state
    halves = range(2)
    du, dv = east(u1), north(v1, first, last)
    h1 = tuple(h1[i] - 0.125 * (du[i] + dv[i]) for i in halves)
    du, dv = east(u2), north(v2, first, last)
    h2 = tuple(h2[i] - 0.0625 * (du[i] + dv[i]) for i in halves)

    def turn(u, v, p):
        px, py = east(p), north(p, first, last)
        return (
            tuple((u[i] + CORIOLIS * v[i] - 0.125 * px[i]) * mask[i] for i in halves),
            tuple((v[i] - CORIOLIS * u[i] - 0.125 * py[i]) * mask[i] for i in halves),
        )

    u1, v1 = turn(u1, v1, tuple(h1[i] + h2[i] for i in halves))
    u2, v2 = turn(u2, v2, tuple(h1[i] + STRATIFY * h2[i] for i in halves))
    return (u1, v1, h1, u2, v2, h2)


def halves_of(x):
    return (x[..., 0:128], x[..., 128:256])


def forecast(state, mask):
    lane = lax.broadcasted_iota(jnp.int32, mask.shape[:1] + (128,), 1)
    first = lane == 0
    last = lane == 127
    state = tuple(halves_of(x) for x in state)
    mask = halves_of(mask)
    for _ in range(2):
        state = step(state, mask, first, last)
    return state


def skew(x, odd, high):
    once = [jnp.where(odd, x[(i + 1) % 4], x[i]) for i in range(4)]
    return [jnp.where(high, once[(i + 2) % 4], once[i]) for i in range(4)]


def swap_blocks(groups):
    lane = lax.broadcasted_iota(jnp.int32, (8, 128), 1)
    odd = (lane & 32) != 0
    high = lane >= 64
    skewed = [skew(x, odd, high) for x in groups]
    turned = [[w[0]] + [pltpu.roll(w[d], 32 * d, 1) for d in range(1, 4)] for w in skewed]
    back = [skew(w, odd, high) for w in turned]
    return [(w[0], w[3], w[2], w[1]) for w in back]


BLOCKS = [(f, qx, g) for f in range(6) for qx in range(2) for g in range(2)]
INNER = 7
INNER_ROWS = 6 * INNER


def edges_kernel(state, land, low_out, high_out, top, bottom, land_top, land_bottom, sems):
    copies = [
        pltpu.make_async_copy(state.at[:, :, 0:8, :], top, sems.at[0]),
        pltpu.make_async_copy(state.at[:, :, 56:64, :], bottom, sems.at[1]),
        pltpu.make_async_copy(land.at[0:8, :], land_top, sems.at[2]),
        pltpu.make_async_copy(land.at[56:64, :], land_bottom, sems.at[3]),
    ]
    for copy in copies:
        copy.start()
    for copy in copies:
        copy.wait()
    low_out[24] = land_bottom[8 - HALO :, :].astype(jnp.float32)
    high_out[24] = land_top[:HALO, :].astype(jnp.float32)
    for m in range(4):
        for f in range(6):
            low_out[6 * m + f] = bottom[m, f, 8 - HALO :, :]
            high_out[6 * m + f] = top[m, f, :HALO, :]


CUTS = (0, 40, 80, 120, 168)


def inner_kernel(state, land, out, begin, land_ref, packed, fields_ref, sems):
    arrive = [pltpu.make_async_copy(land, land_ref, sems.at[0])]
    arrive += [pltpu.make_async_copy(state.at[m], begin.at[m], sems.at[1 + m]) for m in range(4)]
    leave = [
        pltpu.make_async_copy(
            packed.at[:, pl.ds(CUTS[m], CUTS[m + 1] - CUTS[m]), :],
            out.at[:, pl.ds(CUTS[m], CUTS[m + 1] - CUTS[m]), :],
            sems.at[5 + m],
        )
        for m in range(4)
    ]
    for copy in arrive:
        copy.start()
    arrive[0].wait()
    mask = land_ref[...].astype(jnp.float32)
    mask = jnp.concatenate([mask, mask], axis=0)

    def cast(members):
        fields = forecast(
            tuple(jnp.concatenate([begin[m, f] for m in members], axis=0) for f in range(6)), mask
        )
        for m in members:
            for f in range(6):
                for g in range(2):
                    fields_ref[m, f, g] = fields[f][g][64 * (m % 2) : 64 * (m % 2) + 64]

    def pack(m):
        for i in range(0, len(BLOCKS), 12):
            todo = BLOCKS[i : i + 12]
            tiles = swap_blocks(
                [
                    [fields_ref[m, f, g, pl.ds((4, 32)[qx] + a, 8, stride=4), :] for a in range(4)]
                    for f, qx, g in todo
                ]
            )
            for (f, qx, g), z in zip(todo, tiles):
                row = m * INNER_ROWS + f * INNER
                for b in range(4):
                    packed[qx * 8 + g * 4 + b, row : row + INNER, :] = z[b][0:INNER]

    for m in (0, 1):
        arrive[1 + m].wait()
    cast((0, 1))
    for m in (2, 3):
        arrive[1 + m].wait()
    pack(0)
    pack(1)
    cast((2, 3))
    leave[0].start()
    leave[1].start()
    for m in (2, 3):
        pack(m)
        leave[m].start()
    for copy in leave:
        copy.wait()


def outer_kernel(state, land, from_low, from_high, packed, ocean, fields_ref):
    mask = jnp.concatenate(
        [
            land[0:16, :].astype(jnp.float32),
            land[48:64, :].astype(jnp.float32),
            from_high[24],
            from_low[24],
        ],
        axis=0,
    )

    def one(m, carry):
        begin = tuple(
            jnp.concatenate(
                [state[m, f, 0:16, :], state[m, f, 48:64, :], from_high[6 * m + f], from_low[6 * m + f]],
                axis=0,
            )
            for f in range(6)
        )
        fields = forecast(begin, mask)
        for f in range(6):
            for g in range(2):
                sides = jnp.concatenate([fields[f][g][0:4], fields[f][g][28:32]], axis=0)
                fields_ref[g, pl.ds(pl.multiple_of((6 * m + f) * 8, 8), 8), :] = sides
        return carry

    lax.fori_loop(0, 4, one, 0)
    for g in range(2):
        ocean[g] = land[:, 128 * g : 128 * g + 128].astype(jnp.float32)
    todo = [(i, qx, g) for i in range(3) for qx in range(2) for g in range(2)]
    tiles = swap_blocks(
        [
            [fields_ref[g, pl.ds(64 * i + 4 * qx + a, 8, stride=8), :] for a in range(4)]
            for i, qx, g in todo
        ]
    )
    for (i, qx, g), z in zip(todo, tiles):
        for b in range(4):
            packed[qx * 8 + g * 4 + b, 8 * i : 8 * i + 8, :] = z[b]


def places(index, members):
    chosen = index[...]
    side = lax.axis_index("member") // 8
    field = chosen >> 10
    group = ((chosen >> 7) + side) & 7
    row = jnp.where(group == 0, INNER_ROWS + field, field * INNER + group - 1)
    lane = chosen & 127
    halves = [slice(0, 128), slice(128, 256)]
    return (
        [jnp.broadcast_to(row[:, half], (members, 128)) for half in halves],
        [jnp.broadcast_to(lane[:, half], (members, 128)) for half in halves],
    )


def pick(tile, r, rows_of, lanes_of, acc):
    return tuple(
        jnp.where(rows_of[half] == r, jnp.take_along_axis(tile, lanes_of[half], axis=1), acc[half])
        for half in range(2)
    )


def split(x):
    members = x.shape[0]
    dev = x - jnp.sum(x, axis=0, keepdims=True) * (1.0 / members)
    high = dev.astype(jnp.bfloat16)
    return high, (dev - high.astype(jnp.float32)).astype(jnp.bfloat16)


def gather_kernel(x_ref, index, observed, dev_ref):
    members = 64
    rows_of, lanes_of = places(index, members)

    def scan(block, acc):
        rows = [block * SCAN + i for i in range(SCAN)]
        tiles = [x_ref[pl.ds(r, members, stride=INNER_ROWS), :] for r in rows]
        for r, tile in zip(rows, tiles):
            acc = pick(tile, r, rows_of, lanes_of, acc)
        for r, tile in zip(rows, tiles):
            high, low = split(tile)
            dev_ref[r, 0:members, :] = high
            dev_ref[r, members:, :] = low
        return acc

    zero = jnp.zeros((members, 128), jnp.float32)
    acc = lax.fori_loop(0, INNER_ROWS // SCAN, scan, (zero, zero))
    observed[:, 0:128] = acc[0]
    observed[:, 128:256] = acc[1]


def analysis_kernel(
    x_ref, picked, dev_ref, index, count, values, errors, out_ref, outer_ref
):
    members = 64
    rows_of, lanes_of = places(index, members)
    acc = (picked[:, 0:128], picked[:, 128:256])
    for f in range(6):
        tile = x_ref[pl.ds(f, members, stride=6), :]
        acc = pick(tile, INNER_ROWS + f, rows_of, lanes_of, acc)
        high, low = split(tile)
        outer_ref[f, 0:members, :] = high
        outer_ref[f, members:, :] = low
    observed = jnp.concatenate(acc, axis=1)
    obs_mean = jnp.sum(observed, axis=0, keepdims=True) * (1.0 / members)
    spread = observed - obs_mean
    slots = lax.broadcasted_iota(jnp.int32, (1, 256), 1)
    weight = jnp.where(slots < count[...], 1.0 / errors[...], 0.0)
    innovation = values[...] - obs_mean
    scaled = spread * weight
    column = lax.broadcasted_iota(jnp.int32, (members, 2 * members), 1)
    line = lax.broadcasted_iota(jnp.int32, (members, 2 * members), 0)
    twice = (line == (column & (members - 1))).astype(jnp.float32)
    once = (line == column).astype(jnp.float32)

    def parts(a, count=3):
        found = []
        for _ in range(count):
            found.append(a.astype(jnp.bfloat16))
            a = a - found[-1].astype(jnp.float32)
        return found

    nothing = jnp.zeros((members, 2 * members), jnp.bfloat16)

    def times(a, b):
        (ah, am, al), (bh, bm, bl) = a, b
        coarse = jnp.dot(
            jnp.concatenate([ah, am], axis=1),
            jnp.concatenate([bh, bm, bh, bm], axis=0),
            preferred_element_type=jnp.float32,
        )
        fine = jnp.dot(
            jnp.concatenate([al, ah], axis=1),
            jnp.concatenate([bh, bm, bl, nothing], axis=0),
            preferred_element_type=jnp.float32,
        )
        return coarse + fine

    def over_slots(a, b):
        return lax.dot_general(
            a,
            jnp.concatenate([b, b], axis=0),
            (((1,), (1,)), ((), ())),
            preferred_element_type=jnp.float32,
        )

    (ah, am, al), (bh, bm, bl) = parts(scaled), parts(spread)
    gram = over_slots(ah, bh) + (
        (over_slots(ah, bm) + over_slots(am, bh))
        + (over_slots(am, bm) + over_slots(ah, bl) + over_slots(al, bh))
    )
    moved = jnp.sum(once * jnp.sum(scaled * innovation, axis=1, keepdims=True), axis=0, keepdims=True)
    system = (members - 1.0) * twice + gram
    system_parts = parts(system)
    square = times(system_parts, system_parts)
    total = 0.5 * jnp.sum(jnp.sum(system * system, axis=0, keepdims=True), axis=1, keepdims=True)
    norm_inv = lax.rsqrt(total)
    norm_inv_root = jnp.sqrt(norm_inv)
    root = system * norm_inv
    inverse = 1.5 * twice - 0.5 * root
    root = 1.5 * root - 0.5 * (square * norm_inv * norm_inv)
    for sweep in range(1, NS_ITERS):
        root_parts, inverse_parts = parts(root), parts(inverse)
        factor = 1.5 * twice - 0.5 * times(inverse_parts, root_parts)
        factor_parts = parts(factor)
        if sweep < NS_ITERS - 1:
            root = times(root_parts, factor_parts)
            inverse = times(factor_parts, inverse_parts)
    left_half = (column[0:1] < members).astype(jnp.float32)
    weights = moved
    for _ in range(2):
        step_one = jnp.sum(inverse * weights, axis=1, keepdims=True)
        weights = jnp.sum(factor * step_one, axis=0, keepdims=True) * left_half
    weights = weights + pltpu.roll(weights, members, 1)
    sqrt_inv = times(factor_parts, inverse_parts) * norm_inv_root
    flipped = weights * norm_inv + math.sqrt(members - 1.0) * sqrt_inv - twice
    left = jnp.concatenate(parts(flipped, 2), axis=0)

    def apply(pair_of, places_of):
        results = []
        for pair in pair_of:
            both = jnp.dot(left, pair, preferred_element_type=jnp.float32)
            results.append(both[0:members] + both[members:])
        for result, rows in zip(results, places_of):
            for j in range(2):
                out_ref[pl.ds(rows[j], members, stride=48), :] = result[:, 128 * j : 128 * j + 128]

    for i in range(3):
        first = 2 * INNER * i
        pairs = [
            jnp.concatenate([dev_ref[first + 2 * k], dev_ref[first + 2 * k + 1]], axis=1)
            for k in range(INNER)
        ]
        pairs.append(jnp.concatenate([outer_ref[2 * i], outer_ref[2 * i + 1]], axis=1))
        spots = [[r + r // INNER + 1 for r in (first + 2 * k, first + 2 * k + 1)] for k in range(INNER)]
        spots.append([16 * i, 16 * i + 8])
        apply(pairs, spots)


def unpack_kernel(packed, land, out, field, sems):
    copies = [
        pltpu.make_async_copy(field.at[m, :, g], out.at[m, :, :, pl.ds(128 * g, 128)], sems.at[m, g])
        for m in range(4)
        for g in range(2)
    ]
    masks = {}
    for qx in range(2):
        for g in range(2):
            for a in range(4):
                rows = land[g, pl.ds(32 * qx + a, 8, stride=4), :]
                masks[qx, g, a] = rows
    for m in range(4):
        for i in range(0, len(BLOCKS), 12):
            todo = BLOCKS[i : i + 12]
            tiles = swap_blocks(
                [
                    [
                        packed[qx * 8 + g * 4 + b, 48 * m + 8 * f : 48 * m + 8 * f + 8, :]
                        for b in range(4)
                    ]
                    for f, qx, g in todo
                ]
            )
            for (f, qx, g), z in zip(todo, tiles):
                for a in range(4):
                    tile = pltpu.roll(z[a], 7, 0) if qx else z[a]
                    field[m, f, g, pl.ds(32 * qx + a, 8, stride=4), :] = tile * masks[qx, g, a]
        for g in range(2):
            copies[2 * m + g].start()
    for copy in copies:
        copy.wait()


def shape(*dims):
    return jax.ShapeDtypeStruct(dims, jnp.float32)


def local(initial_realizations, land_mask, obs_index, obs_count, obs_value, obs_error):
    whole = pl.BlockSpec(memory_space=pltpu.VMEM)
    far = pl.BlockSpec(memory_space=pltpu.HBM)
    to_high, to_low = pl.pallas_call(
        edges_kernel,
        out_shape=[shape(25, HALO, 256)] * 2,
        in_specs=[far, far],
        out_specs=[whole, whole],
        scratch_shapes=[
            pltpu.VMEM((4, 6, 8, 256), jnp.float32),
            pltpu.VMEM((4, 6, 8, 256), jnp.float32),
            pltpu.VMEM((8, 256), jnp.int32),
            pltpu.VMEM((8, 256), jnp.int32),
            pltpu.SemaphoreType.DMA((4,)),
        ],
        cost_estimate=pl.CostEstimate(flops=100000, bytes_accessed=800000, transcendentals=0),
    )(initial_realizations, land_mask)
    count = lax.axis_size("domain")
    forward = [(i, (i + 1) % count) for i in range(count)]
    backward = [(target, source) for source, target in forward]
    from_low = lax.ppermute(to_high, "domain", forward)
    from_high = lax.ppermute(to_low, "domain", backward)
    inner = pl.pallas_call(
        inner_kernel,
        out_shape=shape(16, 4 * INNER_ROWS, 128),
        in_specs=[far, far],
        out_specs=far,
        scratch_shapes=[
            pltpu.VMEM((4, 6, 64, 256), jnp.float32),
            pltpu.VMEM((64, 256), jnp.int32),
            pltpu.VMEM((16, 4 * INNER_ROWS, 128), jnp.float32),
            pltpu.VMEM((4, 6, 2, 64, 128), jnp.float32),
            pltpu.SemaphoreType.DMA((9,)),
        ],
        compiler_params=pltpu.CompilerParams(vmem_limit_bytes=WHOLE_VMEM),
        cost_estimate=pl.CostEstimate(flops=20000000, bytes_accessed=3000000, transcendentals=0),
    )(initial_realizations, land_mask)
    outer, ocean = pl.pallas_call(
        outer_kernel,
        out_shape=[shape(16, 24, 128), shape(2, 64, 128)],
        in_specs=[whole] * 4,
        out_specs=[whole] * 2,
        scratch_shapes=[pltpu.VMEM((2, 192, 128), jnp.float32)],
        compiler_params=pltpu.CompilerParams(vmem_limit_bytes=VMEM_LIMIT),
        cost_estimate=pl.CostEstimate(flops=10000000, bytes_accessed=3000000, transcendentals=0),
    )(initial_realizations, land_mask, from_low, from_high)
    inner = lax.all_to_all(inner, "member", split_axis=0, concat_axis=0, tiled=True)
    outer = lax.all_to_all(outer, "member", split_axis=0, concat_axis=0, tiled=True)
    observed, deviations = pl.pallas_call(
        gather_kernel,
        out_shape=[shape(64, 256), jax.ShapeDtypeStruct((INNER_ROWS, 128, 128), jnp.bfloat16)],
        in_specs=[whole] * 2,
        out_specs=[whole] * 2,
        compiler_params=pltpu.CompilerParams(vmem_limit_bytes=VMEM_LIMIT),
        cost_estimate=pl.CostEstimate(flops=10000000, bytes_accessed=3000000, transcendentals=0),
    )(inner.reshape(64 * INNER_ROWS, 128), obs_index[0])
    increment = pl.pallas_call(
        analysis_kernel,
        out_shape=shape(3072, 128),
        in_specs=[whole] * 7,
        out_specs=whole,
        scratch_shapes=[pltpu.VMEM((6, 128, 128), jnp.bfloat16)],
        compiler_params=pltpu.CompilerParams(vmem_limit_bytes=VMEM_LIMIT),
        cost_estimate=pl.CostEstimate(flops=60000000, bytes_accessed=3000000, transcendentals=0),
    )(
        outer.reshape(384, 128),
        observed,
        deviations,
        obs_index[0],
        obs_count,
        obs_value[0],
        obs_error[0],
    )
    returned = lax.all_to_all(
        increment.reshape(16, 192, 128), "member", split_axis=0, concat_axis=0, tiled=True
    )
    return pl.pallas_call(
        unpack_kernel,
        out_shape=shape(4, 6, 64, 256),
        in_specs=[whole, whole],
        out_specs=far,
        scratch_shapes=[pltpu.VMEM((4, 6, 2, 64, 128), jnp.float32), pltpu.SemaphoreType.DMA((4, 2))],
        compiler_params=pltpu.CompilerParams(vmem_limit_bytes=VMEM_LIMIT),
    )(returned, ocean)


def solution(mesh):
    in_specs = (
        P("member", None, "domain", None),
        P("domain", None),
        P("domain", "member", None),
        P("domain", "member"),
        P("domain", "member", None),
        P("domain", "member", None),
    )
    out_specs = P("member", None, "domain", None)
    return jax.shard_map(local, mesh=mesh, in_specs=in_specs, out_specs=out_specs, check_vma=False)
```

```python
import math

import jax
import jax.numpy as jnp
from jax import lax
from jax.experimental import pallas as pl
from jax.experimental.pallas import tpu as pltpu
from jax.sharding import PartitionSpec as P

NS_ITERS = 8
CORIOLIS = 0.1
STRATIFY = 1.5
HALO = 4
SCAN = 14
VMEM_LIMIT = 48 * 1024 * 1024
WHOLE_VMEM = 62 * 1024 * 1024


def east(field):
    return tuple(pltpu.roll(x, x.shape[0] - 1, 0) - pltpu.roll(x, 1, 0) for x in field)


def north(field, first, last):
    west, rest = field
    west_up, rest_up = pltpu.roll(west, 1, 1), pltpu.roll(rest, 1, 1)
    west_down, rest_down = pltpu.roll(west, 127, 1), pltpu.roll(rest, 127, 1)
    return (
        jnp.where(last, rest_down, west_down) - jnp.where(first, 0.0, west_up),
        jnp.where(last, 0.0, rest_down) - jnp.where(first, west_up, rest_up),
    )


def step(state, mask, first, last):
    u1, v1, h1, u2, v2, h2 = state
    halves = range(2)
    du, dv = east(u1), north(v1, first, last)
    h1 = tuple(h1[i] - 0.125 * (du[i] + dv[i]) for i in halves)
    du, dv = east(u2), north(v2, first, last)
    h2 = tuple(h2[i] - 0.0625 * (du[i] + dv[i]) for i in halves)

    def turn(u, v, p):
        px, py = east(p), north(p, first, last)
        return (
            tuple((u[i] + CORIOLIS * v[i] - 0.125 * px[i]) * mask[i] for i in halves),
            tuple((v[i] - CORIOLIS * u[i] - 0.125 * py[i]) * mask[i] for i in halves),
        )

    u1, v1 = turn(u1, v1, tuple(h1[i] + h2[i] for i in halves))
    u2, v2 = turn(u2, v2, tuple(h1[i] + STRATIFY * h2[i] for i in halves))
    return (u1, v1, h1, u2, v2, h2)


def halves_of(x):
    return (x[..., 0:128], x[..., 128:256])


def forecast(state, mask):
    lane = lax.broadcasted_iota(jnp.int32, mask.shape[:1] + (128,), 1)
    first = lane == 0
    last = lane == 127
    state = tuple(halves_of(x) for x in state)
    mask = halves_of(mask)
    for _ in range(2):
        state = step(state, mask, first, last)
    return state


def skew(x, odd, high):
    once = [jnp.where(odd, x[(i + 1) % 4], x[i]) for i in range(4)]
    return [jnp.where(high, once[(i + 2) % 4], once[i]) for i in range(4)]


def swap_blocks(groups):
    lane = lax.broadcasted_iota(jnp.int32, (8, 128), 1)
    odd = (lane & 32) != 0
    high = lane >= 64
    skewed = [skew(x, odd, high) for x in groups]
    turned = [[w[0]] + [pltpu.roll(w[d], 32 * d, 1) for d in range(1, 4)] for w in skewed]
    back = [skew(w, odd, high) for w in turned]
    return [(w[0], w[3], w[2], w[1]) for w in back]


BLOCKS = [(f, qx, g) for f in range(6) for qx in range(2) for g in range(2)]
INNER = 7
INNER_ROWS = 6 * INNER


def edges_kernel(state, land, low_out, high_out, top, bottom, land_top, land_bottom, sems):
    copies = [
        pltpu.make_async_copy(state.at[:, :, 0:8, :], top, sems.at[0]),
        pltpu.make_async_copy(state.at[:, :, 56:64, :], bottom, sems.at[1]),
        pltpu.make_async_copy(land.at[0:8, :], land_top, sems.at[2]),
        pltpu.make_async_copy(land.at[56:64, :], land_bottom, sems.at[3]),
    ]
    for copy in copies:
        copy.start()
    for copy in copies:
        copy.wait()
    low_out[24] = land_bottom[8 - HALO :, :].astype(jnp.float32)
    high_out[24] = land_top[:HALO, :].astype(jnp.float32)
    for m in range(4):
        for f in range(6):
            low_out[6 * m + f] = bottom[m, f, 8 - HALO :, :]
            high_out[6 * m + f] = top[m, f, :HALO, :]


CUTS = (0, 40, 80, 120, 168)


def inner_kernel(state, land, out, begin, land_ref, packed, fields_ref, sems):
    arrive = [pltpu.make_async_copy(land, land_ref, sems.at[0])]
    arrive += [pltpu.make_async_copy(state.at[m], begin.at[m], sems.at[1 + m]) for m in range(4)]
    leave = [
        pltpu.make_async_copy(
            packed.at[:, pl.ds(CUTS[m], CUTS[m + 1] - CUTS[m]), :],
            out.at[:, pl.ds(CUTS[m], CUTS[m + 1] - CUTS[m]), :],
            sems.at[5 + m],
        )
        for m in range(4)
    ]
    for copy in arrive:
        copy.start()
    arrive[0].wait()
    mask = land_ref[...].astype(jnp.float32)
    mask = jnp.concatenate([mask, mask], axis=0)

    def cast(members):
        fields = forecast(
            tuple(jnp.concatenate([begin[m, f] for m in members], axis=0) for f in range(6)), mask
        )
        for m in members:
            for f in range(6):
                for g in range(2):
                    fields_ref[m, f, g] = fields[f][g][64 * (m % 2) : 64 * (m % 2) + 64]

    def pack(m):
        for i in range(0, len(BLOCKS), 12):
            todo = BLOCKS[i : i + 12]
            tiles = swap_blocks(
                [
                    [fields_ref[m, f, g, pl.ds((4, 32)[qx] + a, 8, stride=4), :] for a in range(4)]
                    for f, qx, g in todo
                ]
            )
            for (f, qx, g), z in zip(todo, tiles):
                row = m * INNER_ROWS + f * INNER
                for b in range(4):
                    packed[qx * 8 + g * 4 + b, row : row + INNER, :] = z[b][0:INNER]

    for m in (0, 1):
        arrive[1 + m].wait()
    cast((0, 1))
    for m in (2, 3):
        arrive[1 + m].wait()
    pack(0)
    pack(1)
    cast((2, 3))
    leave[0].start()
    leave[1].start()
    for m in (2, 3):
        pack(m)
        leave[m].start()
    for copy in leave:
        copy.wait()


def outer_kernel(state, land, from_low, from_high, packed, ocean, fields_ref):
    mask = jnp.concatenate(
        [
            land[0:16, :].astype(jnp.float32),
            land[48:64, :].astype(jnp.float32),
            from_high[24],
            from_low[24],
        ],
        axis=0,
    )

    def one(m, carry):
        begin = tuple(
            jnp.concatenate(
                [state[m, f, 0:16, :], state[m, f, 48:64, :], from_high[6 * m + f], from_low[6 * m + f]],
                axis=0,
            )
            for f in range(6)
        )
        fields = forecast(begin, mask)
        for f in range(6):
            for g in range(2):
                sides = jnp.concatenate([fields[f][g][0:4], fields[f][g][28:32]], axis=0)
                fields_ref[g, pl.ds(pl.multiple_of((6 * m + f) * 8, 8), 8), :] = sides
        return carry

    lax.fori_loop(0, 4, one, 0)
    for g in range(2):
        ocean[g] = land[:, 128 * g : 128 * g + 128].astype(jnp.float32)
    todo = [(i, qx, g) for i in range(3) for qx in range(2) for g in range(2)]
    tiles = swap_blocks(
        [
            [fields_ref[g, pl.ds(64 * i + 4 * qx + a, 8, stride=8), :] for a in range(4)]
            for i, qx, g in todo
        ]
    )
    for (i, qx, g), z in zip(todo, tiles):
        for b in range(4):
            packed[qx * 8 + g * 4 + b, 8 * i : 8 * i + 8, :] = z[b]


def places(index, members):
    chosen = index[...]
    side = lax.axis_index("member") // 8
    field = chosen >> 10
    group = ((chosen >> 7) + side) & 7
    row = jnp.where(group == 0, INNER_ROWS + field, field * INNER + group - 1)
    lane = chosen & 127
    halves = [slice(0, 128), slice(128, 256)]
    return (
        [jnp.broadcast_to(row[:, half], (members, 128)) for half in halves],
        [jnp.broadcast_to(lane[:, half], (members, 128)) for half in halves],
    )


def pick(tile, r, rows_of, lanes_of, acc):
    return tuple(
        jnp.where(rows_of[half] == r, jnp.take_along_axis(tile, lanes_of[half], axis=1), acc[half])
        for half in range(2)
    )


def split(x):
    members = x.shape[0]
    dev = x - jnp.sum(x, axis=0, keepdims=True) * (1.0 / members)
    high = dev.astype(jnp.bfloat16)
    return high, (dev - high.astype(jnp.float32)).astype(jnp.bfloat16)


def gather_kernel(x_ref, index, observed, dev_ref):
    members = 64
    rows_of, lanes_of = places(index, members)

    def scan(block, acc):
        rows = [block * SCAN + i for i in range(SCAN)]
        tiles = [x_ref[pl.ds(r, members, stride=INNER_ROWS), :] for r in rows]
        for r, tile in zip(rows, tiles):
            acc = pick(tile, r, rows_of, lanes_of, acc)
        for r, tile in zip(rows, tiles):
            high, low = split(tile)
            dev_ref[r, 0:members, :] = high
            dev_ref[r, members:, :] = low
        return acc

    zero = jnp.zeros((members, 128), jnp.float32)
    acc = lax.fori_loop(0, INNER_ROWS // SCAN, scan, (zero, zero))
    observed[:, 0:128] = acc[0]
    observed[:, 128:256] = acc[1]


def analysis_kernel(
    x_ref, picked, dev_ref, index, count, values, errors, out_ref, outer_ref
):
    members = 64
    rows_of, lanes_of = places(index, members)
    acc = (picked[:, 0:128], picked[:, 128:256])
    for f in range(6):
        tile = x_ref[pl.ds(f, members, stride=6), :]
        acc = pick(tile, INNER_ROWS + f, rows_of, lanes_of, acc)
        high, low = split(tile)
        outer_ref[f, 0:members, :] = high
        outer_ref[f, members:, :] = low
    observed = jnp.concatenate(acc, axis=1)
    obs_mean = jnp.sum(observed, axis=0, keepdims=True) * (1.0 / members)
    spread = observed - obs_mean
    slots = lax.broadcasted_iota(jnp.int32, (1, 256), 1)
    weight = jnp.where(slots < count[...], 1.0 / errors[...], 0.0)
    innovation = values[...] - obs_mean
    scaled = spread * weight
    column = lax.broadcasted_iota(jnp.int32, (members, 2 * members), 1)
    line = lax.broadcasted_iota(jnp.int32, (members, 2 * members), 0)
    twice = (line == (column & (members - 1))).astype(jnp.float32)
    once = (line == column).astype(jnp.float32)

    def parts(a, count=3):
        found = []
        for _ in range(count):
            found.append(a.astype(jnp.bfloat16))
            a = a - found[-1].astype(jnp.float32)
        return found

    nothing = jnp.zeros((members, 2 * members), jnp.bfloat16)

    def times(a, b):
        (ah, am, al), (bh, bm, bl) = a, b
        coarse = jnp.dot(
            jnp.concatenate([ah, am], axis=1),
            jnp.concatenate([bh, bm, bh, bm], axis=0),
            preferred_element_type=jnp.float32,
        )
        fine = jnp.dot(
            jnp.concatenate([al, ah], axis=1),
            jnp.concatenate([bh, bm, bl, nothing], axis=0),
            preferred_element_type=jnp.float32,
        )
        return coarse + fine

    def over_slots(a, b):
        return jnp.dot(a, b, preferred_element_type=jnp.float32)

    ah, am, al = parts(scaled)
    bh, bm, bl = parts(jnp.concatenate([spread, spread], axis=0).T)
    first = over_slots(jnp.concatenate([ah, am, al], axis=0), bh)
    second = over_slots(jnp.concatenate([ah, am], axis=0), bm)
    gram = first[0:members] + (
        (first[members : 2 * members] + second[0:members])
        + (first[2 * members :] + second[members:] + over_slots(ah, bl))
    )
    moved = jnp.sum(once * jnp.sum(scaled * innovation, axis=1, keepdims=True), axis=0, keepdims=True)
    system = (members - 1.0) * twice + gram
    system_parts = parts(system)
    square = times(system_parts, system_parts)
    total = 0.5 * jnp.sum(jnp.sum(system * system, axis=0, keepdims=True), axis=1, keepdims=True)
    norm_inv = lax.rsqrt(total)
    norm_inv_root = jnp.sqrt(norm_inv)
    root = system * norm_inv
    inverse = 1.5 * twice - 0.5 * root
    root = 1.5 * root - 0.5 * (square * norm_inv * norm_inv)
    for sweep in range(1, NS_ITERS):
        root_parts, inverse_parts = parts(root), parts(inverse)
        factor = 1.5 * twice - 0.5 * times(inverse_parts, root_parts)
        factor_parts = parts(factor)
        if sweep < NS_ITERS - 1:
            root = times(root_parts, factor_parts)
            inverse = times(factor_parts, inverse_parts)
    left_half = (column[0:1] < members).astype(jnp.float32)
    weights = moved
    for _ in range(2):
        step_one = jnp.sum(inverse * weights, axis=1, keepdims=True)
        weights = jnp.sum(factor * step_one, axis=0, keepdims=True) * left_half
    weights = weights + pltpu.roll(weights, members, 1)
    sqrt_inv = times(factor_parts, inverse_parts) * norm_inv_root
    flipped = weights * norm_inv + math.sqrt(members - 1.0) * sqrt_inv - twice
    left = jnp.concatenate(parts(flipped, 2), axis=0)

    def apply(pair_of, places_of):
        results = []
        for pair in pair_of:
            both = jnp.dot(left, pair, preferred_element_type=jnp.float32)
            results.append(both[0:members] + both[members:])
        for result, rows in zip(results, places_of):
            for j in range(2):
                out_ref[pl.ds(rows[j], members, stride=48), :] = result[:, 128 * j : 128 * j + 128]

    for i in range(3):
        first = 2 * INNER * i
        pairs = [
            jnp.concatenate([dev_ref[first + 2 * k], dev_ref[first + 2 * k + 1]], axis=1)
            for k in range(INNER)
        ]
        pairs.append(jnp.concatenate([outer_ref[2 * i], outer_ref[2 * i + 1]], axis=1))
        spots = [[r + r // INNER + 1 for r in (first + 2 * k, first + 2 * k + 1)] for k in range(INNER)]
        spots.append([16 * i, 16 * i + 8])
        apply(pairs, spots)


def unpack_kernel(packed, land, out, field, sems):
    copies = [
        pltpu.make_async_copy(field.at[m, :, g], out.at[m, :, :, pl.ds(128 * g, 128)], sems.at[m, g])
        for m in range(4)
        for g in range(2)
    ]
    masks = {}
    for qx in range(2):
        for g in range(2):
            for a in range(4):
                rows = land[g, pl.ds(32 * qx + a, 8, stride=4), :]
                masks[qx, g, a] = rows
    for m in range(4):
        for i in range(0, len(BLOCKS), 12):
            todo = BLOCKS[i : i + 12]
            tiles = swap_blocks(
                [
                    [
                        packed[qx * 8 + g * 4 + b, 48 * m + 8 * f : 48 * m + 8 * f + 8, :]
                        for b in range(4)
                    ]
                    for f, qx, g in todo
                ]
            )
            for (f, qx, g), z in zip(todo, tiles):
                for a in range(4):
                    tile = pltpu.roll(z[a], 7, 0) if qx else z[a]
                    field[m, f, g, pl.ds(32 * qx + a, 8, stride=4), :] = tile * masks[qx, g, a]
        for g in range(2):
            copies[2 * m + g].start()
    for copy in copies:
        copy.wait()


def shape(*dims):
    return jax.ShapeDtypeStruct(dims, jnp.float32)


def local(initial_realizations, land_mask, obs_index, obs_count, obs_value, obs_error):
    whole = pl.BlockSpec(memory_space=pltpu.VMEM)
    far = pl.BlockSpec(memory_space=pltpu.HBM)
    to_high, to_low = pl.pallas_call(
        edges_kernel,
        out_shape=[shape(25, HALO, 256)] * 2,
        in_specs=[far, far],
        out_specs=[whole, whole],
        scratch_shapes=[
            pltpu.VMEM((4, 6, 8, 256), jnp.float32),
            pltpu.VMEM((4, 6, 8, 256), jnp.float32),
            pltpu.VMEM((8, 256), jnp.int32),
            pltpu.VMEM((8, 256), jnp.int32),
            pltpu.SemaphoreType.DMA((4,)),
        ],
        cost_estimate=pl.CostEstimate(flops=100000, bytes_accessed=800000, transcendentals=0),
    )(initial_realizations, land_mask)
    count = lax.axis_size("domain")
    forward = [(i, (i + 1) % count) for i in range(count)]
    backward = [(target, source) for source, target in forward]
    from_low = lax.ppermute(to_high, "domain", forward)
    from_high = lax.ppermute(to_low, "domain", backward)
    inner = pl.pallas_call(
        inner_kernel,
        out_shape=shape(16, 4 * INNER_ROWS, 128),
        in_specs=[far, far],
        out_specs=far,
        scratch_shapes=[
            pltpu.VMEM((4, 6, 64, 256), jnp.float32),
            pltpu.VMEM((64, 256), jnp.int32),
            pltpu.VMEM((16, 4 * INNER_ROWS, 128), jnp.float32),
            pltpu.VMEM((4, 6, 2, 64, 128), jnp.float32),
            pltpu.SemaphoreType.DMA((9,)),
        ],
        compiler_params=pltpu.CompilerParams(vmem_limit_bytes=WHOLE_VMEM),
        cost_estimate=pl.CostEstimate(flops=20000000, bytes_accessed=3000000, transcendentals=0),
    )(initial_realizations, land_mask)
    outer, ocean = pl.pallas_call(
        outer_kernel,
        out_shape=[shape(16, 24, 128), shape(2, 64, 128)],
        in_specs=[whole] * 4,
        out_specs=[whole] * 2,
        scratch_shapes=[pltpu.VMEM((2, 192, 128), jnp.float32)],
        compiler_params=pltpu.CompilerParams(vmem_limit_bytes=VMEM_LIMIT),
        cost_estimate=pl.CostEstimate(flops=10000000, bytes_accessed=3000000, transcendentals=0),
    )(initial_realizations, land_mask, from_low, from_high)
    inner = lax.all_to_all(inner, "member", split_axis=0, concat_axis=0, tiled=True)
    outer = lax.all_to_all(outer, "member", split_axis=0, concat_axis=0, tiled=True)
    observed, deviations = pl.pallas_call(
        gather_kernel,
        out_shape=[shape(64, 256), jax.ShapeDtypeStruct((INNER_ROWS, 128, 128), jnp.bfloat16)],
        in_specs=[whole] * 2,
        out_specs=[whole] * 2,
        compiler_params=pltpu.CompilerParams(vmem_limit_bytes=VMEM_LIMIT),
        cost_estimate=pl.CostEstimate(flops=10000000, bytes_accessed=3000000, transcendentals=0),
    )(inner.reshape(64 * INNER_ROWS, 128), obs_index[0])
    increment = pl.pallas_call(
        analysis_kernel,
        out_shape=shape(3072, 128),
        in_specs=[whole] * 7,
        out_specs=whole,
        scratch_shapes=[pltpu.VMEM((6, 128, 128), jnp.bfloat16)],
        compiler_params=pltpu.CompilerParams(vmem_limit_bytes=VMEM_LIMIT),
        cost_estimate=pl.CostEstimate(flops=60000000, bytes_accessed=3000000, transcendentals=0),
    )(
        outer.reshape(384, 128),
        observed,
        deviations,
        obs_index[0],
        obs_count,
        obs_value[0],
        obs_error[0],
    )
    returned = lax.all_to_all(
        increment.reshape(16, 192, 128), "member", split_axis=0, concat_axis=0, tiled=True
    )
    return pl.pallas_call(
        unpack_kernel,
        out_shape=shape(4, 6, 64, 256),
        in_specs=[whole, whole],
        out_specs=far,
        scratch_shapes=[pltpu.VMEM((4, 6, 2, 64, 128), jnp.float32), pltpu.SemaphoreType.DMA((4, 2))],
        compiler_params=pltpu.CompilerParams(vmem_limit_bytes=VMEM_LIMIT),
    )(returned, ocean)


def solution(mesh):
    in_specs = (
        P("member", None, "domain", None),
        P("domain", None),
        P("domain", "member", None),
        P("domain", "member"),
        P("domain", "member", None),
        P("domain", "member", None),
    )
    out_specs = P("member", None, "domain", None)
    return jax.shard_map(local, mesh=mesh, in_specs=in_specs, out_specs=out_specs, check_vma=False)
```
